256 devices in a mesh: stream: 2 (over core), depth: 4 (over z_lo), height: 32 (over z_hi, x, y).
Axes of the slice: x: 4, y: 4, z: 8 (z_hi: 2, z_lo: 4; z = z_hi * 4 + z_lo), core: 2. Of those that a mesh axis runs over, the one named last changes fastest.
Arguments:
- tokens: bfloat16 [2, 40, 320, 1920], P('stream', 'depth', 'height'), may hold values from -40 to 40
- ln_gain: float32 [192], replicated, may hold values from 0.1 to 1.9
- w_query: bfloat16 [192, 192], replicated, may hold values from -0.4375 to 0.4375
- w_keyval: bfloat16 [192, 384], replicated, may hold values from -0.4375 to 0.4375
- w_out: bfloat16 [192, 192], replicated, may hold values from -0.4375 to 0.4375
- w_merge: bfloat16 [1536, 384], replicated, may hold values from -0.15625 to 0.15625
- owner_map: int32 [4, 32], P('depth', 'height'), may hold values from 0 to 31, as said below
- relay_grad: bfloat16 [2, 384, 48000], P('stream', ('depth', 'height')), may hold values from -6 to 6
Outputs:
- relayed: bfloat16 [2, 384, 48000], P('stream', ('depth', 'height'))
- token_grad: bfloat16 [2, 40, 320, 1920], P('stream', 'depth', 'height')
- gain_grad: float32 [192], replicated
- query_wgrad: float32 [192, 192], replicated
- keyval_wgrad: float32 [192, 384], replicated
- out_wgrad: float32 [192, 192], replicated
- merge_wgrad: float32 [1536, 384], replicated
The draws below stay inside these ranges and needn't reach their ends.
Inputs may be any that keep to these rules, and one draw needn't show every extreme that they name: `owner_map`: entry j of row r names the height index of the owner of next-section window j of depth row r: with h = j // 1 the height index that formed it, the owner is h - 1, h or h + 1, taken modulo 32. Every owner receives at most 3 windows, and in every depth row some owner receives exactly 3, all 1 windows of each of its two neighbours among them.
All inputs are finite; a program needn't handle non-finite values.
Results may differ from the reference program's by a relative error of at most 0.0081.
The reference program's roundings to bfloat16 on the way count: a program that leaves them out, or rounds other values in their place, can miss the bound.
Values may be sent and summed in bfloat16 or wider, within the bound.
A program may use at most 128 MiB of HBM per device.

```python
import math
import jax
import jax.numpy as jnp
from jax import lax

C = 192
HEADS = 6
HEAD_DIM = 32
WID = 10
DEPTH = 40
HEIGHT = 320
TOKENS = 128000
WIN_DEV = 1
CAP = 3
PAYLOAD = 48000
N_DEPTH = 4
N_HEIGHT = 32


def draw_tokens(key, part):
    key = jax.random.fold_in(key, 11)
    normal_key, row_key, column_key = jax.random.split(key, 3)
    cell_shape = (2, DEPTH, HEIGHT, WID, C)
    raw_values = jnp.clip(jax.random.normal(normal_key, cell_shape, jnp.float32), -4.0, 4.0)
    row_scale = jnp.exp(jax.random.uniform(row_key, cell_shape[:4] + (1,), jnp.float32, math.log(0.25), math.log(2.5)))
    column_scale = jnp.exp(jax.random.uniform(column_key, (C,), jnp.float32, math.log(0.4), math.log(4.0)))
    return jnp.clip(raw_values * row_scale * column_scale, -40.0, 40.0).reshape(2, DEPTH, HEIGHT, WID * C).astype(jnp.bfloat16)


def owner_row(key):
    hot_key, pattern_key = jax.random.split(key, 2)
    hottest = jax.random.randint(hot_key, (), 0, N_HEIGHT, jnp.int32)
    heights = jnp.arange(N_HEIGHT, dtype=jnp.int32)
    steps = jax.random.randint(pattern_key, (N_HEIGHT, WIN_DEV), 0, 3, jnp.int32)
    column = heights[:, None]
    steps = jnp.where(column == (hottest + N_HEIGHT - 1) % N_HEIGHT, 2, steps)
    steps = jnp.where(column == hottest, 1, steps)
    steps = jnp.where(column == (hottest + 1) % N_HEIGHT, 0, steps)
    owners = (column + steps - 1 + N_HEIGHT) % N_HEIGHT
    return owners.reshape(N_HEIGHT * WIN_DEV).astype(jnp.int32)


def draw_owner_map(key, part):
    key = jax.random.fold_in(key, 23)
    return jax.vmap(owner_row)(jax.random.split(key, N_DEPTH)).astype(jnp.int32)


def block_scale(own_key, dims, shards, least, top_value):
    def one(axis_at, parts):
        steps = jax.random.uniform(jax.random.fold_in(jax.random.fold_in(own_key, 6), axis_at), (parts,), jnp.float32, least / len(shards), top_value / len(shards))
        return jnp.repeat(jnp.exp(steps), dims[axis_at] // parts).reshape((-1,) + (1,) * (len(dims) - axis_at - 1))

    factor_of = one(*shards[0])
    for cut in shards[1:]:
        factor_of = factor_of * one(*cut)
    return factor_of


def noise(own_key, dims, spread, bound, cuts=(), kind=jnp.bfloat16):
    entries = spread * jax.random.normal(own_key, dims, jnp.float32)
    if cuts:
        entries = entries * block_scale(own_key, dims, cuts, -0.22, 0.18)
    return jnp.clip(entries, -bound, bound).astype(kind)


def setup_inputs(seed: int = 0) -> dict:
    arg_keys = jax.random.split(jax.random.key(seed), 9)
    tokens = draw_tokens(jax.random.fold_in(arg_keys[8], 71), 0)
    ln_gain = jnp.clip(1.0 + 0.18 * jax.random.normal(arg_keys[1], (C,), jnp.float32), 0.1, 1.9)
    w_query = noise(arg_keys[2], (C, C), C ** -0.5, 0.4375)
    w_keyval = noise(arg_keys[3], (C, 2 * C), C ** -0.5, 0.4375)
    w_out = noise(arg_keys[4], (C, C), C ** -0.5, 0.4375)
    w_merge = noise(arg_keys[5], (8 * C, 2 * C), (8 * C) ** -0.5, 0.15625)
    owner_map = draw_owner_map(jax.random.fold_in(arg_keys[8], 71), 0)
    relay_grad = noise(arg_keys[7], (2, N_DEPTH * N_HEIGHT * CAP, PAYLOAD), 1.0, 6.0, ((0, 2), (1, 128)))
    return {"tokens": tokens, "ln_gain": ln_gain, "w_query": w_query, "w_keyval": w_keyval, "w_out": w_out, "w_merge": w_merge, "owner_map": owner_map, "relay_grad": relay_grad}


norm_epsilon = 1e-05

def normalize(values):
    centre = lax.optimization_barrier(jnp.mean(values, -1, keepdims=True))
    shifted = values - centre
    inverse = lax.rsqrt(lax.optimization_barrier(jnp.mean(shifted * shifted, -1, keepdims=True)) + norm_epsilon)
    return shifted * inverse

def normalize_back(values, upstream):
    centre = lax.optimization_barrier(jnp.mean(values, -1, keepdims=True))
    shifted = values - centre
    inverse = lax.rsqrt(lax.optimization_barrier(jnp.mean(shifted * shifted, -1, keepdims=True)) + norm_epsilon)
    normed = shifted * inverse
    return inverse * (upstream - lax.optimization_barrier(jnp.mean(upstream, -1, keepdims=True)) - normed * lax.optimization_barrier(jnp.mean(upstream * normed, -1, keepdims=True)))

def rounded(values):
    return lax.optimization_barrier(values.astype(jnp.bfloat16)).astype(jnp.float32)

def window_rims(tensor, axis_pos, number):
    leading = jnp.moveaxis(tensor, axis_pos, 0)
    middle = leading[1:number * 5 + 1].reshape((number, 5) + leading.shape[1:])
    before = leading[0:number * 5:5][:, None]
    after_rim = leading[6:number * 5 + 2:5][:, None]
    joined = jnp.concatenate([before, middle, after_rim], 1)
    return jnp.moveaxis(joined, (0, 1), (axis_pos, axis_pos + 1))

def gather_search(region, depth_count, height_count, width_count):
    feature = region.shape[-1]
    search = window_rims(region, 0, depth_count)
    search = window_rims(search, 2, height_count)
    search = window_rims(search, 4, width_count)
    search = jnp.transpose(search, (0, 2, 4, 1, 3, 5, 6))
    return search.reshape(depth_count * height_count * width_count, 343, feature)

def base_windows(volume):
    depth_count, height_count, width_count = (volume.shape[0] // 5, volume.shape[1] // 5, volume.shape[2] // 5)
    feature = volume.shape[3]
    pieces = volume.reshape(depth_count, 5, height_count, 5, width_count, 5, feature)
    pieces = jnp.transpose(pieces, (0, 2, 4, 1, 3, 5, 6))
    return pieces.reshape(depth_count * height_count * width_count, 125, feature)

def window_grid(windows, depth_count, height_count, width_count):
    feature = windows.shape[-1]
    pieces = windows.reshape(depth_count, height_count, width_count, 5, 5, 5, feature)
    pieces = jnp.transpose(pieces, (0, 3, 1, 4, 2, 5, 6))
    return pieces.reshape(depth_count * 5, height_count * 5, width_count * 5, feature)

def to_eight(volume):
    leading_dims = volume.shape[:-4]
    depth_len, height, width_len, feature = volume.shape[-4:]
    offset = len(leading_dims)
    pieces = volume.reshape(leading_dims + (depth_len // 2, 2, height // 2, 2, width_len // 2, 2, feature))
    order_dims = tuple(range(offset)) + (offset, offset + 2, offset + 4, offset + 1, offset + 3, offset + 5, offset + 6)
    return jnp.transpose(pieces, order_dims).reshape(leading_dims + (depth_len // 2, height // 2, width_len // 2, 8 * feature))

def from_eight(volume, feature):
    leading_dims = volume.shape[:-4]
    depth_half, height_half, width_half = volume.shape[-4:-1]
    offset = len(leading_dims)
    pieces = volume.reshape(leading_dims + (depth_half, height_half, width_half, 2, 2, 2, feature))
    order_dims = tuple(range(offset)) + (offset, offset + 3, offset + 1, offset + 4, offset + 2, offset + 5, offset + 6)
    return jnp.transpose(pieces, order_dims).reshape(leading_dims + (2 * depth_half, 2 * height_half, 2 * width_half, feature))

def next_windows(volume):
    leading_dims = volume.shape[:-4]
    depth_half, height_half, width_half, feature = volume.shape[-4:]
    offset = len(leading_dims)
    pieces = volume.reshape(leading_dims + (depth_half // 5, 5, height_half // 5, 5, width_half // 5, 5, feature))
    order_dims = tuple(range(offset)) + (offset, offset + 2, offset + 4, offset + 1, offset + 3, offset + 5, offset + 6)
    return jnp.transpose(pieces, order_dims).reshape(leading_dims + (depth_half // 5, height_half // 5, width_half // 5, 125 * feature))

def next_grid(windows, feature):
    leading_dims = windows.shape[:-4]
    depth_blocks, height_blocks, width_blocks = windows.shape[-4:-1]
    offset = len(leading_dims)
    pieces = windows.reshape(leading_dims + (depth_blocks, height_blocks, width_blocks, 5, 5, 5, feature))
    order_dims = tuple(range(offset)) + (offset, offset + 3, offset + 1, offset + 4, offset + 2, offset + 5, offset + 6)
    return jnp.transpose(pieces, order_dims).reshape(leading_dims + (5 * depth_blocks, 5 * height_blocks, 5 * width_blocks, feature))

def in_blocks(function, arrays, block_size):
    window_total = arrays[0].shape[0]
    grouped = tuple((member.reshape((window_total // block_size, block_size) + member.shape[1:]) for member in arrays))
    result = lax.map(lambda pieces: function(*pieces), grouped)
    return jax.tree.map(lambda stacked: stacked.reshape((window_total,) + stacked.shape[2:]), result)

def score_block(query_w, keyval_w, inside_keys):
    windows = query_w.shape[0]
    query_heads = query_w.astype(jnp.float32).reshape(windows, 125, HEADS, HEAD_DIM)
    key_heads = keyval_w[:, :, :C].astype(jnp.float32).reshape(windows, 343, HEADS, HEAD_DIM)
    value_heads = keyval_w[:, :, C:].astype(jnp.float32).reshape(windows, 343, HEADS, HEAD_DIM)
    scores = jnp.einsum('nqhd,nkhd->nhqk', query_heads, key_heads, precision=lax.Precision.HIGHEST) * HEAD_DIM ** (-0.5)
    weights = jnp.exp(scores) * inside_keys[:, None, None, :]
    attention = weights / lax.optimization_barrier(jnp.sum(weights, -1, keepdims=True))
    return (attention, query_heads, key_heads, value_heads)

def attend_forward(query_w, keyval_w, inside_keys):
    attention, query_heads, key_heads, value_heads = score_block(query_w, keyval_w, inside_keys)
    context = jnp.einsum('nhqk,nkhd->nqhd', rounded(attention), value_heads, precision=lax.Precision.HIGHEST)
    return context.reshape(query_w.shape)

def attend_backward(query_w, keyval_w, inside_keys, context_grad):
    attention, query_heads, key_heads, value_heads = score_block(query_w, keyval_w, inside_keys)
    attention_r = rounded(attention)
    windows = query_w.shape[0]
    grad_heads = context_grad.astype(jnp.float32).reshape(windows, 125, HEADS, HEAD_DIM)
    weight_grad = jnp.einsum('nqhd,nkhd->nhqk', grad_heads, value_heads, precision=lax.Precision.HIGHEST)
    value_grad = jnp.einsum('nhqk,nqhd->nkhd', attention_r, grad_heads, precision=lax.Precision.HIGHEST)
    score_grad = rounded(attention_r * (weight_grad - lax.optimization_barrier(jnp.sum(weight_grad * attention_r, -1, keepdims=True))) * HEAD_DIM ** (-0.5))
    query_grad = jnp.einsum('nhqk,nkhd->nqhd', score_grad, key_heads, precision=lax.Precision.HIGHEST)
    key_grad = jnp.einsum('nhqk,nqhd->nkhd', score_grad, query_heads, precision=lax.Precision.HIGHEST)
    return (query_grad.reshape(windows, 125, C), jnp.concatenate([key_grad, value_grad], 2).reshape(windows, 343, 2 * C))

def reference(tokens, ln_gain, w_query, w_keyval, w_out, w_merge, owner_map, relay_grad):
    row_total = DEPTH // 5
    height_count = HEIGHT // 5
    width_count = WID // 5
    block_size = math.gcd(height_count * width_count, 64)
    values = tokens.reshape(2, DEPTH, HEIGHT, WID, C).astype(jnp.float32)
    normed = normalize(values)
    normal_rows = (normed * ln_gain).astype(jnp.bfloat16).reshape(-1, C)
    query_cells = jnp.dot(normal_rows, w_query, preferred_element_type=jnp.float32).astype(jnp.bfloat16).reshape(2, DEPTH, HEIGHT, WID, C)
    keyval = jnp.dot(normal_rows, w_keyval, preferred_element_type=jnp.float32).astype(jnp.bfloat16).reshape(2, DEPTH, HEIGHT, WID, 2 * C)
    padded = jnp.pad(keyval[::-1], ((0, 0), (1, 1), (1, 1), (1, 1), (0, 0)))
    inside = jnp.pad(jnp.ones((DEPTH, HEIGHT, WID, 1), jnp.float32), ((1, 1), (1, 1), (1, 1), (0, 0)))
    anchor = jnp.zeros((), jnp.int32)

    def row_parts(row_index):
        stream_index = row_index // row_total
        row_start = row_index % row_total * 5
        region = lax.dynamic_slice(padded, (stream_index, row_start, anchor, anchor, anchor), (1, 7, HEIGHT + 2, WID + 2, 2 * C))[0]
        inside_region = lax.dynamic_slice(inside, (row_start, anchor, anchor, anchor), (7, HEIGHT + 2, WID + 2, 1))
        query_slab = lax.dynamic_slice(query_cells, (stream_index, row_start, anchor, anchor, anchor), (1, 5, HEIGHT, WID, C))[0]
        inside_keys = gather_search(inside_region, 1, height_count, width_count)[:, :, 0]
        return (base_windows(query_slab), gather_search(region, 1, height_count, width_count), inside_keys)

    def forward_row(row_index):
        query_w, keyval_w, inside_keys = row_parts(row_index)
        return in_blocks(attend_forward, (query_w, keyval_w, inside_keys), block_size).astype(jnp.bfloat16)
    row_ids = jnp.arange(2 * row_total, dtype=jnp.int32)
    context_w = lax.map(forward_row, row_ids)
    context = jax.vmap(lambda member: window_grid(member, 1, height_count, width_count))(context_w).reshape(2, DEPTH, HEIGHT, WID, C)
    context_rows = context.reshape(-1, C)
    output = (jnp.dot(context_rows, w_out, preferred_element_type=jnp.float32).reshape(values.shape) + values).astype(jnp.bfloat16)
    eight_cells = to_eight(output).reshape(-1, 8 * C)
    merged = jnp.dot(eight_cells, w_merge, preferred_element_type=jnp.float32).astype(jnp.bfloat16)
    window_rows = next_windows(merged.reshape(2, DEPTH // 2, HEIGHT // 2, WID // 2, 2 * C)).reshape(2, N_DEPTH, N_HEIGHT * WIN_DEV, PAYLOAD)
    window_order = jnp.arange(N_HEIGHT * WIN_DEV, dtype=jnp.int32)
    earlier = (owner_map[:, :, None] == owner_map[:, None, :]) & (window_order[None, None, :] < window_order[None, :, None])
    rank_index = lax.optimization_barrier(jnp.sum(earlier.astype(jnp.int32), -1))
    slot_index = owner_map * CAP + rank_index
    depth_rows = jnp.arange(N_DEPTH, dtype=jnp.int32)[:, None]
    relayed = jnp.zeros((2, N_DEPTH, N_HEIGHT * CAP, PAYLOAD), jnp.bfloat16).at[:, depth_rows, slot_index].set(window_rows)
    grad_rows = relay_grad.reshape(2, N_DEPTH, N_HEIGHT * CAP, PAYLOAD)[:, depth_rows, slot_index]
    merged_grad = next_grid(grad_rows.reshape(2, N_DEPTH, HEIGHT // 10, WID // 10, PAYLOAD), 2 * C).reshape(-1, 2 * C)
    merge_sum = jnp.dot(eight_cells.T, merged_grad, preferred_element_type=jnp.float32)
    eight_grad = jnp.dot(merged_grad, w_merge.T, preferred_element_type=jnp.float32).astype(jnp.bfloat16)
    output_grad = from_eight(eight_grad.reshape(2, DEPTH // 2, HEIGHT // 2, WID // 2, 8 * C), C).reshape(-1, C)
    out_sum = jnp.dot(context_rows.T, output_grad, preferred_element_type=jnp.float32)
    context_grad = jnp.dot(output_grad, w_out.T, preferred_element_type=jnp.float32).astype(jnp.bfloat16).reshape(2, DEPTH, HEIGHT, WID, C)

    def backward_row(keyval_total, row_index):
        query_w, keyval_w, inside_keys = row_parts(row_index)
        stream_index = row_index // row_total
        row_start = row_index % row_total * 5
        slab_grad = lax.dynamic_slice(context_grad, (stream_index, row_start, anchor, anchor, anchor), (1, 5, HEIGHT, WID, C))[0]
        query_wgrad_w, keyval_wgrad_w = in_blocks(attend_backward, (query_w, keyval_w, inside_keys, base_windows(slab_grad)), block_size)
        _, spread_back = jax.vjp(lambda region: gather_search(region, 1, height_count, width_count), jnp.zeros((7, HEIGHT + 2, WID + 2, 2 * C), jnp.float32))
        region_grad = spread_back(keyval_wgrad_w)[0]
        corner = (stream_index, row_start, anchor, anchor, anchor)
        current = lax.dynamic_slice(keyval_total, corner, (1, 7, HEIGHT + 2, WID + 2, 2 * C))
        keyval_total = lax.dynamic_update_slice(keyval_total, current + region_grad[None], corner)
        return (keyval_total, window_grid(query_wgrad_w, 1, height_count, width_count).astype(jnp.bfloat16))
    keyval_start = jnp.zeros((2, DEPTH + 2, HEIGHT + 2, WID + 2, 2 * C), jnp.float32)
    keyval_total, query_slabs = lax.scan(backward_row, keyval_start, row_ids)
    query_grad = query_slabs.reshape(-1, C)
    keyval_grad = keyval_total[:, 1:-1, 1:-1, 1:-1][::-1].astype(jnp.bfloat16).reshape(-1, 2 * C)
    norm_grad = jnp.dot(query_grad, w_query.T, preferred_element_type=jnp.float32) + jnp.dot(keyval_grad, w_keyval.T, preferred_element_type=jnp.float32)
    query_sum = jnp.dot(normal_rows.T, query_grad, preferred_element_type=jnp.float32)
    keyval_sum = jnp.dot(normal_rows.T, keyval_grad, preferred_element_type=jnp.float32)
    norm_grad = norm_grad.reshape(values.shape)
    gain_sum = lax.optimization_barrier(jnp.sum((norm_grad * normed).reshape(-1, C), 0))
    token_grad = (normalize_back(values, norm_grad * ln_gain) + output_grad.reshape(values.shape).astype(jnp.float32)).astype(jnp.bfloat16)
    grad_scale = (2.0 * TOKENS) ** (-0.5)
    return (relayed.reshape(2, N_DEPTH * N_HEIGHT * CAP, PAYLOAD), token_grad.reshape(tokens.shape), gain_sum * grad_scale, query_sum * grad_scale, keyval_sum * grad_scale, out_sum * grad_scale, merge_sum * grad_scale)
```

```python
import functools

import jax
import jax.numpy as jnp
import numpy as np
from jax import lax
from jax.experimental import pallas as pl
from jax.experimental.pallas import tpu as pltpu
from jax.sharding import PartitionSpec as P

C = 192
HEADS = 6
EPS = 1e-05
N_DEPTH = 4
N_HEIGHT = 32
SCALE = 32 ** (-0.5)
EXP2_SCALE = SCALE * 1.4426950408889634
MESH = pl.DeviceIdType.MESH
F32 = jnp.float32
BF16 = jnp.bfloat16
VM = pl.BlockSpec(memory_space=pltpu.VMEM)
SM = pl.BlockSpec(memory_space=pltpu.SMEM)
LIMIT = 56 * 1024 * 1024


def dot(a, b):
    return lax.dot_general(a, b, (((1,), (0,)), ((), ())), preferred_element_type=F32)


def dot_nt(a, b):
    return lax.dot_general(a, b, (((1,), (1,)), ((), ())), preferred_element_type=F32)


def dot_tn(a, b):
    return lax.dot_general(a, b, (((0,), (0,)), ((), ())), preferred_element_type=F32)


def place():
    return lax.axis_index("stream"), lax.axis_index("depth"), lax.axis_index("height")


def neighbours():
    s, d, h = place()
    dl, dh = lax.rem(d + N_DEPTH - 1, N_DEPTH), lax.rem(d + 1, N_DEPTH)
    hl, hh = lax.rem(h + N_HEIGHT - 1, N_HEIGHT), lax.rem(h + 1, N_HEIGHT)
    o = 1 - s
    return {
        "p": (o, d, h),
        "dl": (o, dl, h),
        "dh": (o, dh, h),
        "hl": (o, d, hl),
        "hh": (o, d, hh),
        "ll": (o, dl, hl),
        "lh": (o, dl, hh),
        "hdl": (o, dh, hl),
        "hdh": (o, dh, hh),
        "sl": (s, d, hl),
        "sh": (s, d, hh),
    }


def greet(peers):
    barrier = pltpu.get_barrier_semaphore()
    for peer in peers:
        pl.semaphore_signal(barrier, inc=1, device_id=peer, device_id_type=MESH)
    pl.semaphore_wait(barrier, len(peers))


def copier(send_sem, recv_sem):
    def make(src, dst, index, peer):
        return pltpu.make_async_remote_copy(
            src_ref=src,
            dst_ref=dst,
            send_sem=send_sem.at[index],
            recv_sem=recv_sem.at[index],
            device_id=peer,
            device_id_type=MESH,
        )

    return make


def relay_ranks(fl, fs, fr):
    _, _, h = place()
    left, right = lax.rem(h + N_HEIGHT - 1, N_HEIGHT), lax.rem(h + 1, N_HEIGHT)

    def before(a, b):
        return jnp.where(a < b, 1, 0)

    rank_l = fs * before(h, left) + fr * before(right, left)
    rank_s = fl * before(left, h) + fr * before(right, h)
    rank_r = fl * before(left, right) + fs * before(h, right)
    return rank_l, rank_s, rank_r


def wide(row):
    return jnp.concatenate([row, row, row], axis=1)


def intake_kernel(
    tok, rg, own, own_tok, region, rims, corners, merged_grad, owners,
    stage, hstage, hsend, rows, mg_send, mg_recv, own_send, send_sem, recv_sem,
):
    _, _, h = place()
    peers = neighbours()
    copy = copier(send_sem, recv_sem)
    own_send[...] = jnp.full((8, 128), own[0, 0], jnp.int32)
    greet(list(peers.values()))
    to_left = copy(own_send, owners.at[2], 0, peers["sl"])
    to_right = copy(own_send, owners.at[0], 1, peers["sh"])
    to_left.start()
    to_right.start()
    owners[1] = own_send[...]
    stage[...] = jnp.zeros_like(stage)
    hstage[...] = jnp.zeros_like(hstage)
    for d in range(10):
        x = tok[d].astype(F32)
        stage[d, 1:7, :] = x[0:6]
        stage[d, 9:14, :] = x[5:10]
        stage[d, 8:9, :] = x[4:5]
        hstage[0, d : d + 1, :] = x[0:1]
        hstage[1, d : d + 1, :] = x[9:10]
    own_tok[...] = stage[...].astype(BF16)
    hsend[...] = hstage[...].astype(BF16)
    copies = [
        copy(own_tok, region.at[pl.ds(1, 10)], 2, peers["p"]),
        copy(own_tok.at[9], region.at[0], 3, peers["dh"]),
        copy(own_tok.at[0], region.at[11], 4, peers["dl"]),
        copy(hsend.at[1], rims.at[0], 5, peers["hh"]),
        copy(hsend.at[0], rims.at[1], 6, peers["hl"]),
        copy(own_tok.at[9], corners.at[0], 7, peers["hdh"]),
        copy(own_tok.at[9], corners.at[1], 8, peers["hdl"]),
        copy(own_tok.at[0], corners.at[2], 9, peers["lh"]),
        copy(own_tok.at[0], corners.at[3], 10, peers["ll"]),
    ]
    for one in copies:
        one.start()
    rows[...] = jnp.zeros_like(rows)

    def spread(i, carry):
        x = rg[:, pl.ds(pl.multiple_of(i * 384, 128), 384)].astype(F32)
        for k in range(3):
            rows[k, pl.ds(i, 1), :] = x[k : k + 1]
        return carry

    lax.fori_loop(0, 125, spread, 0)
    to_left.wait()
    to_right.wait()
    fl = jnp.where(owners[0, 0:1, :] == h, 1, 0)
    fs = jnp.where(owners[1, 0:1, :] == h, 1, 0)
    fr = jnp.where(owners[2, 0:1, :] == h, 1, 0)
    rank_l, rank_s, rank_r = relay_ranks(fl, fs, fr)

    def pick(rank):
        rank = wide(rank)
        return jnp.where(rank == 0, rows[0], jnp.where(rank == 1, rows[1], rows[2]))

    mg_send[0] = pick(rank_l).astype(BF16)
    mg_send[1] = pick(rank_r).astype(BF16)
    back_left = copy(mg_send.at[0], mg_recv.at[1], 11, peers["sl"])
    back_right = copy(mg_send.at[1], mg_recv.at[0], 12, peers["sh"])
    back_left.start()
    back_right.start()
    mine = pick(rank_s)
    left, right = lax.rem(h + N_HEIGHT - 1, N_HEIGHT), lax.rem(h + 1, N_HEIGHT)
    target = wide(owners[1, 0:1, :])
    back_left.wait()
    back_right.wait()
    merged_grad[...] = jnp.where(
        target == left,
        mg_recv[0].astype(F32),
        jnp.where(target == right, mg_recv[1].astype(F32), mine),
    ).astype(BF16)
    for one in copies:
        one.wait()


def intake(tok, rg, own):
    return pl.pallas_call(
        intake_kernel,
        out_shape=(
            jax.ShapeDtypeStruct((10, 16, 1920), BF16),
            jax.ShapeDtypeStruct((12, 16, 1920), BF16),
            jax.ShapeDtypeStruct((2, 16, 1920), BF16),
            jax.ShapeDtypeStruct((4, 16, 1920), BF16),
            jax.ShapeDtypeStruct((128, 384), BF16),
            jax.ShapeDtypeStruct((3, 8, 128), jnp.int32),
        ),
        in_specs=[VM, VM, SM],
        out_specs=(VM,) * 6,
        scratch_shapes=[
            pltpu.VMEM((10, 16, 1920), F32),
            pltpu.VMEM((2, 16, 1920), F32),
            pltpu.VMEM((2, 16, 1920), BF16),
            pltpu.VMEM((3, 128, 384), F32),
            pltpu.VMEM((2, 128, 384), BF16),
            pltpu.VMEM((2, 128, 384), BF16),
            pltpu.VMEM((8, 128), jnp.int32),
            pltpu.SemaphoreType.DMA((13,)),
            pltpu.SemaphoreType.DMA((13,)),
        ],
        compiler_params=pltpu.CompilerParams(
            collective_id=1, has_side_effects=True, vmem_limit_bytes=LIMIT
        ),
        name="intake",
    )(tok, rg, own)


def normalized(x):
    centre = jnp.mean(x, -1, keepdims=True)
    shifted = x - centre
    inverse = lax.rsqrt(jnp.mean(shifted * shifted, -1, keepdims=True) + EPS)
    return shifted * inverse, inverse


def eight_index(window, q):
    wi, di, hi = window // 4, (window // 2) % 2, window % 2
    a = (q * 41) >> 10
    rest = q - a * 25
    b = (rest * 205) >> 10
    c = rest - b * 5
    w, d, h = a + 5 * wi, b + 5 * di, c + 5 * hi
    offset = ((d & 1) * 2 + (h & 1)) * 2 + (w & 1)
    cell = ((d >> 1) * 5 + (h >> 1)) * 5 + (w >> 1)
    return jnp.where(q < 125, offset * 128 + cell, -1)


def compute_kernel(
    own_tok, region, rims, corners, mg, gain, wq, wkv, wo, wm, g, gt,
    merged, gm, go, qg_n, og_n, kv_main, kv_d, kv_h, kv_c,
    reg, qreg, xreg, kreg, vreg, acck, accv, og_e, out_w, pt, qbd, qbd_t, cgbd, cgbd_t,
    ctx_t, qg_t, cstage, wk, wv,
):
    _, dep, hei = place()
    slot = lax.broadcasted_iota(jnp.int32, (16, 1920), 0)
    for d in range(12):
        v = region[d].astype(F32)
        if d == 0:
            lo, hi = corners[0].astype(F32)[13:14], corners[1].astype(F32)[1:2]
        elif d == 11:
            lo, hi = corners[2].astype(F32)[13:14], corners[3].astype(F32)[1:2]
        else:
            lo = rims[0].astype(F32)[d - 1 : d]
            hi = rims[1].astype(F32)[d - 1 : d]
        reg[d] = jnp.where(slot == 0, lo, jnp.where(slot == 14, hi, v))
    row = lax.broadcasted_iota(jnp.int32, (192, 256), 0)
    lane = lax.broadcasted_iota(jnp.int32, (192, 256), 1)
    rd, rs = row >> 4, row & 15
    outside = (
        ((rd == 0) & (dep == 0))
        | ((rd == 11) & (dep == N_DEPTH - 1))
        | ((rs == 0) & (hei == 0))
        | ((rs == 14) & (hei == N_HEIGHT - 1))
        | ((rs & 7) == 7)
    )
    bias = jnp.where(outside & (lane == 192), -1e30, 0.0)
    edge = jnp.where(lane == 192, -1e30, 0.0).reshape(12, 16, 256)
    gains = gain[...]
    wk[...] = jnp.zeros_like(wk)
    wk[:, :C] = wkv[:, :C]
    wv[...] = wkv[:, C:]
    for pair in range(5):
        lanes = slice(384 * pair, 384 * pair + 384)
        own2 = own_tok[:, :, lanes].astype(F32).reshape(160, 384)
        reg2 = reg[:, :, lanes].reshape(192, 384)
        for half in range(2):
            w = 2 * pair + half
            x = own2[:, 192 * half : 192 * half + 192]
            normal = (normalized(x)[0] * gains).astype(BF16)
            qreg[w] = dot(normal, wq[...]).reshape(10, 16, C)
            xreg[w] = x.reshape(10, 16, C)
            y = reg2[:, 192 * half : 192 * half + 192]
            normal = (normalized(y)[0] * gains).astype(BF16)
            kreg[w + 1] = (dot(normal, wk[...]) + bias).reshape(12, 16, 256)
            vreg[w + 1] = dot(normal, wv[...]).reshape(12, 16, C)
    for w in (0, 11):
        kreg[w] = edge
        vreg[w] = jnp.zeros((12, 16, C), F32)
    acck[...] = jnp.zeros_like(acck)
    accv[...] = jnp.zeros_like(accv)
    for o in range(8):
        og_e[128 * o : 128 * o + 128, :] = dot_nt(
            mg[...], wm[192 * o : 192 * o + 192, :]
        ).astype(BF16)
    qbd_t[...] = jnp.zeros_like(qbd_t)
    cgbd_t[...] = jnp.zeros_like(cgbd_t)
    ones = lax.broadcasted_iota(jnp.int32, (64, 768), 0)
    qbd_t[192:256, :] = jnp.where(ones == 0, 1.0, 0.0).astype(BF16)
    go[...] = jnp.zeros_like(go)
    head = lax.broadcasted_iota(jnp.int32, (128, C), 1) >> 5

    def window(i, carry):
        wi, di, hi = i // 4, (i // 2) % 2, i % 2
        hs = pl.ds(pl.multiple_of(hi * 8, 8), 8)
        cells = (pl.ds(wi * 5, 5), pl.ds(di * 5 + 0, 5), hs)
        around = (pl.ds(wi * 5, 7), pl.ds(di * 5, 7), hs)
        q_w = dot(gt[...], qreg[(*cells, slice(None))].reshape(200, C).astype(BF16))
        x_w = dot(gt[...], xreg[(*cells, slice(None))].reshape(200, C).astype(BF16))
        q = lax.broadcasted_iota(jnp.int32, (128, 1024), 0)
        col = lax.broadcasted_iota(jnp.int32, (128, 1024), 1)
        pick = jnp.where(eight_index(i, q) == col, 1.0, 0.0).astype(BF16)
        q = lax.broadcasted_iota(jnp.int32, (1024, 128), 1)
        col = lax.broadcasted_iota(jnp.int32, (1024, 128), 0)
        pt[i] = jnp.where(eight_index(i, q) == col, 1.0, 0.0).astype(BF16)
        og_w = dot(pick, og_e[...])
        og_b = og_w.astype(BF16)
        cg_w = dot_nt(og_b, wo[...]).astype(BF16).astype(F32)
        q_t = q_w.T.astype(BF16)
        cg_t = cg_w.T.astype(BF16)
        for m in range(HEADS):
            r, l = slice(32 * m, 32 * m + 32), slice(128 * m, 128 * m + 128)
            qbd_t[r, l] = q_t[r]
            cgbd_t[r, l] = cg_t[r]
            qbd[l, :] = jnp.where(head == m, q_w, 0.0).astype(BF16)
            cgbd[l, :] = jnp.where(head == m, cg_w, 0.0).astype(BF16)
        k32 = kreg[(*around, slice(None))].reshape(392, 256)
        v32 = vreg[(*around, slice(None))].reshape(392, C)
        k, v = k32.astype(BF16), v32.astype(BF16)
        k_t = k32[:, :C].T.astype(BF16)
        v_t = v32.T.astype(BF16)
        kg = jnp.zeros((392, C), F32)
        vg = jnp.zeros((392, C), F32)
        for p in range(3):
            l = slice(256 * p, 256 * p + 256)
            e = jnp.exp2(dot(k, qbd_t[:, l]) * EXP2_SCALE)
            a = (e * (1.0 / jnp.sum(e, 0, keepdims=True))).astype(BF16)
            af = a.astype(F32)
            c = dot(v_t[64 * p : 64 * p + 64], a)
            ctx_t[64 * p : 64 * p + 32, :] = c[:32, :128]
            ctx_t[64 * p + 32 : 64 * p + 64, :] = c[32:, 128:]
            wg = dot(v, cgbd_t[:, l])
            total = jnp.sum(wg * af, 0, keepdims=True)
            sg = (af * (wg - total) * SCALE).astype(BF16)
            vg = vg + dot(a, cgbd[l, :])
            kg = kg + dot(sg, qbd[l, :])
            c = dot(k_t[64 * p : 64 * p + 64], sg)
            qg_t[64 * p : 64 * p + 32, :] = c[:32, :128]
            qg_t[64 * p + 32 : 64 * p + 64, :] = c[32:, 128:]
        acck[(*around, slice(None))] += kg.reshape(7, 7, 8, C)
        accv[(*around, slice(None))] += vg.reshape(7, 7, 8, C)
        c_t = ctx_t[...]
        go[...] += dot(c_t.astype(BF16), og_b)
        c_w = c_t.T.astype(BF16)
        out_w[pl.ds(pl.multiple_of(i * 128, 128), 128), :] = (dot(c_w, wo[...]) + x_w).astype(BF16)
        qg_w = qg_t[...].T.astype(BF16)
        qg_n[(*cells, slice(None))] = dot(g[...], qg_w).reshape(5, 5, 8, C)
        og_n[(*cells, slice(None))] = dot(g[...], og_b).reshape(5, 5, 8, C)
        return carry

    lax.fori_loop(0, 8, window, 0)
    out_e = dot(pt[0], out_w[0:128, :])
    for i in range(1, 8):
        out_e = out_e + dot(pt[i], out_w[128 * i : 128 * i + 128, :])
    out_b = out_e.astype(BF16)
    total = jnp.zeros((128, 384), F32)
    for o in range(8):
        part = out_b[128 * o : 128 * o + 128]
        total = total + dot(part, wm[192 * o : 192 * o + 192, :])
        gm[192 * o : 192 * o + 192, :] = dot_tn(part, mg[...]).astype(BF16)
    merged[...] = total.astype(BF16)

    slot = lax.broadcasted_iota(jnp.int32, (12, 16, 384), 1)
    inner = (slot & 7 >= 1) & (slot & 7 <= 5)
    srow = lax.broadcasted_iota(jnp.int32, (16, 192), 0)
    scol = lax.broadcasted_iota(jnp.int32, (16, 192), 1)
    low = jnp.where(scol == srow * 16, 1.0, 0.0).astype(BF16)
    high = jnp.where(scol == srow * 16 + 14, 1.0, 0.0).astype(BF16)
    cstage[...] = jnp.zeros_like(cstage)
    for w in range(10):
        t = jnp.concatenate([acck[w + 1], accv[w + 1]], axis=-1)
        flat = t.reshape(192, 384).astype(BF16)
        lo, hi = dot(low, flat), dot(high, flat)
        kv_h[0, w] = lo.astype(BF16)
        kv_h[1, w] = hi.astype(BF16)
        cstage[0, w : w + 1, :] = lo[0:1]
        cstage[1, w : w + 1, :] = hi[0:1]
        cstage[2, w : w + 1, :] = lo[11:12]
        cstage[3, w : w + 1, :] = hi[11:12]
        t = t + jnp.where(slot == 5, t[:, 8:9, :], jnp.where(slot == 9, t[:, 6:7, :], 0.0))
        b = jnp.where(inner, t, 0.0).astype(BF16)
        kv_main[w] = b[1:11]
        kv_d[0, w] = b[0]
        kv_d[1, w] = b[11]
    kv_c[...] = cstage[...].astype(BF16)


def compute(own_tok, region, rims, corners, mg, gain, wq, wkv, wo, wm):
    g = np.zeros((200, 128), np.float32)
    for a in range(5):
        for b in range(5):
            for c in range(5):
                g[(a * 5 + b) * 8 + c + 1, a * 25 + b * 5 + c] = 1
    g = jnp.asarray(g, BF16)
    return pl.pallas_call(
        compute_kernel,
        out_shape=(
            jax.ShapeDtypeStruct((128, 384), BF16),
            jax.ShapeDtypeStruct((1536, 384), BF16),
            jax.ShapeDtypeStruct((C, C), F32),
            jax.ShapeDtypeStruct((10, 10, 16, C), F32),
            jax.ShapeDtypeStruct((10, 10, 16, C), F32),
            jax.ShapeDtypeStruct((10, 10, 16, 384), BF16),
            jax.ShapeDtypeStruct((2, 10, 16, 384), BF16),
            jax.ShapeDtypeStruct((2, 10, 16, 384), BF16),
            jax.ShapeDtypeStruct((4, 16, 384), BF16),
        ),
        in_specs=[VM] * 12,
        out_specs=(VM,) * 9,
        scratch_shapes=[
            pltpu.VMEM((12, 16, 1920), F32),
            pltpu.VMEM((10, 10, 16, C), F32),
            pltpu.VMEM((10, 10, 16, C), F32),
            pltpu.VMEM((12, 12, 16, 256), F32),
            pltpu.VMEM((12, 12, 16, C), F32),
            pltpu.VMEM((12, 12, 16, C), F32),
            pltpu.VMEM((12, 12, 16, C), F32),
            pltpu.VMEM((1024, C), BF16),
            pltpu.VMEM((1024, C), BF16),
            pltpu.VMEM((8, 1024, 128), BF16),
            pltpu.VMEM((768, C), BF16),
            pltpu.VMEM((256, 768), BF16),
            pltpu.VMEM((768, C), BF16),
            pltpu.VMEM((C, 768), BF16),
            pltpu.VMEM((C, 128), F32),
            pltpu.VMEM((C, 128), F32),
            pltpu.VMEM((4, 16, 384), F32),
            pltpu.VMEM((C, 256), BF16),
            pltpu.VMEM((C, C), BF16),
        ],
        compiler_params=pltpu.CompilerParams(vmem_limit_bytes=LIMIT),
        name="compute",
    )(own_tok, region, rims, corners, mg, gain, wq, wkv, wo, wm, g, g.T)


def exchange_kernel(
    main, kd, kh, kc, merged, r_main, r_d, r_h, r_c, r_merged, send_sem, recv_sem
):
    peers = neighbours()
    copy = copier(send_sem, recv_sem)
    greet(list(peers.values()))
    copies = [
        copy(main, r_main, 0, peers["p"]),
        copy(kd.at[0], r_d.at[1], 1, peers["dl"]),
        copy(kd.at[1], r_d.at[0], 2, peers["dh"]),
        copy(kh.at[0], r_h.at[1], 3, peers["hl"]),
        copy(kh.at[1], r_h.at[0], 4, peers["hh"]),
        copy(kc.at[0], r_c.at[3], 5, peers["ll"]),
        copy(kc.at[1], r_c.at[2], 6, peers["lh"]),
        copy(kc.at[2], r_c.at[1], 7, peers["hdl"]),
        copy(kc.at[3], r_c.at[0], 8, peers["hdh"]),
        copy(merged, r_merged.at[1], 9, peers["sl"]),
        copy(merged, r_merged.at[0], 10, peers["sh"]),
    ]
    for one in copies:
        one.start()
    for one in copies:
        one.wait()


def exchange(main, kd, kh, kc, merged):
    return pl.pallas_call(
        exchange_kernel,
        out_shape=(
            jax.ShapeDtypeStruct((10, 10, 16, 384), BF16),
            jax.ShapeDtypeStruct((2, 10, 16, 384), BF16),
            jax.ShapeDtypeStruct((2, 10, 16, 384), BF16),
            jax.ShapeDtypeStruct((4, 16, 384), BF16),
            jax.ShapeDtypeStruct((2, 128, 384), BF16),
        ),
        in_specs=[VM] * 5,
        out_specs=(VM,) * 5,
        scratch_shapes=[pltpu.SemaphoreType.DMA((11,)), pltpu.SemaphoreType.DMA((11,))],
        compiler_params=pltpu.CompilerParams(
            collective_id=2, has_side_effects=True, vmem_limit_bytes=LIMIT
        ),
        name="exchange",
    )(main, kd, kh, kc, merged)


def finish_kernel(
    own_tok, qg, og, main, rd, rh, rc, merged, r_merged, owners, gain, wq, wkv, go,
    token_grad, relayed, small,
    normals, kvs, qgs, stage, stage2, wins, wide_out,
):
    _, _, h = place()
    gains = gain[...]
    slot = lax.broadcasted_iota(jnp.int32, (16, 384), 0)
    gain_sum = jnp.zeros((1, C), F32)
    for pair in range(5):
        lanes = slice(384 * pair, 384 * pair + 384)
        own2 = own_tok[:, :, lanes].astype(F32).reshape(160, 384)
        grads = []
        for half in range(2):
            w = 2 * pair + half
            lo, hi = rh[0, w].astype(F32), rh[1, w].astype(F32)
            planes = []
            for d in range(10):
                lo_d, hi_d = lo[d + 1 : d + 2], hi[d + 1 : d + 2]
                if d == 0:
                    lo_d = lo_d + rc[0].astype(F32)[w : w + 1]
                    hi_d = hi_d + rc[1].astype(F32)[w : w + 1]
                if d == 9:
                    lo_d = lo_d + rc[2].astype(F32)[w : w + 1]
                    hi_d = hi_d + rc[3].astype(F32)[w : w + 1]
                t = main[w, d].astype(F32)
                t = t + jnp.where(slot == 1, lo_d, jnp.where(slot == 13, hi_d, 0.0))
                if d == 0:
                    t = t + rd[0, w].astype(F32)
                if d == 9:
                    t = t + rd[1, w].astype(F32)
                planes.append(t.astype(BF16))
            kv_b = jnp.concatenate(planes, axis=0)
            qg_b = qg[w].reshape(160, C).astype(BF16)
            rows = slice(160 * w, 160 * w + 160)
            kvs[rows, :] = kv_b
            qgs[rows, :] = qg_b
            x = own2[:, 192 * half : 192 * half + 192]
            normed, inverse = normalized(x)
            normals[rows, :] = (normed * gains).astype(BF16)
            ng = dot_nt(qg_b, wq[...]) + dot_nt(kv_b, wkv[...])
            gain_sum = gain_sum + jnp.sum(ng * normed, 0, keepdims=True)
            u = ng * gains
            grads.append(
                inverse
                * (
                    u
                    - jnp.mean(u, -1, keepdims=True)
                    - normed * jnp.mean(u * normed, -1, keepdims=True)
                )
                + og[w].reshape(160, C)
            )
        stage[:, :, lanes] = jnp.concatenate(grads, axis=1).reshape(10, 16, 384)
    for d in range(10):
        x = stage[d]
        stage2[d, 0:5, :] = x[1:6]
        stage2[d, 5:10, :] = x[9:14]
    token_grad[...] = stage2[...].astype(BF16)
    small[...] = jnp.zeros_like(small)
    small[0:192, :] = dot_tn(normals[...], kvs[...]).astype(BF16)
    small[192:384, :] = jnp.concatenate([dot_tn(normals[...], qgs[...]), go[...]], axis=1).astype(
        BF16
    )
    first = lax.broadcasted_iota(jnp.int32, (16, 384), 0)
    spread = jnp.concatenate([gain_sum, jnp.zeros((1, C), F32)], axis=1)
    small[384:400, :] = jnp.where(first == 0, spread, 0.0).astype(BF16)

    fl = jnp.where(owners[0, 0:1, :] == h, 1, 0)
    fs = jnp.where(owners[1, 0:1, :] == h, 1, 0)
    fr = jnp.where(owners[2, 0:1, :] == h, 1, 0)
    ranks = relay_ranks(fl, fs, fr)
    parts = []
    for flag, rank, win in zip((fl, fs, fr), ranks, (r_merged[0], merged[...], r_merged[1])):
        parts.append((wide(jnp.where(flag == 1, rank, -1)), win.astype(F32)))
    for k in range(3):
        total = jnp.zeros((128, 384), F32)
        for key, win in parts:
            total = jnp.where(key == k, win, total)
        wins[k] = total

    def lay(i, carry):
        lanes = pl.ds(pl.multiple_of(i * 384, 128), 384)
        for k in range(3):
            wide_out[k : k + 1, lanes] = wins[k, pl.ds(i, 1), :]
        return carry

    lax.fori_loop(0, 125, lay, 0)
    relayed[...] = wide_out[...].astype(BF16)


def finish(own_tok, qg, og, main, rd, rh, rc, merged, r_merged, owners, gain, wq, wkv, go):
    return pl.pallas_call(
        finish_kernel,
        out_shape=(
            jax.ShapeDtypeStruct((10, 10, 1920), BF16),
            jax.ShapeDtypeStruct((3, 48000), BF16),
            jax.ShapeDtypeStruct((512, 384), BF16),
        ),
        in_specs=[VM] * 14,
        out_specs=(VM,) * 3,
        scratch_shapes=[
            pltpu.VMEM((1600, C), BF16),
            pltpu.VMEM((1600, 384), BF16),
            pltpu.VMEM((1600, C), BF16),
            pltpu.VMEM((10, 16, 1920), F32),
            pltpu.VMEM((10, 10, 1920), F32),
            pltpu.VMEM((3, 128, 384), F32),
            pltpu.VMEM((3, 48000), F32),
        ],
        compiler_params=pltpu.CompilerParams(vmem_limit_bytes=LIMIT),
        name="finish",
    )(own_tok, qg, og, main, rd, rh, rc, merged, r_merged, owners, gain, wq, wkv, go)


def add_up_kernel(
    gm, sm, out_g, out_s,
    acc, snd2, snd3, snd4, fin, acc2, acc3, r1, r2, r3, r4, res2, res3, res4,
    s_send, s_recv, z_send, z_recv,
):
    s, d, h = place()
    zh, xy = h // 16, lax.rem(h, 16)
    x, y = xy // 4, lax.rem(xy, 4)
    z = zh * 4 + d
    partner = (1 - s, d, h)
    xs = [(s, d, zh * 16 + lax.rem(x + k, 4) * 4 + y) for k in (1, 2, 3)]
    ys = [(s, d, zh * 16 + x * 4 + lax.rem(y + k, 4)) for k in (1, 2, 3)]
    xk = [lax.rem(x + k, 4) for k in (1, 2, 3)]
    yk = [lax.rem(y + k, 4) for k in (1, 2, 3)]
    zk = [lax.rem(z + k, 8) for k in range(1, 8)]
    zs = [(s, lax.rem(t, 4), (t // 4) * 16 + xy) for t in zk]
    copy = copier(s_send, s_recv)
    greet([partner] + xs + ys + zs)

    def run(copies):
        for one in copies:
            one.start()
        for one in copies:
            one.wait()

    o = 1 - s
    run([
        copy(gm.at[pl.ds(48 * o, 48)], r1.at[pl.ds(0, 48)], 0, partner),
        copy(sm.at[pl.ds(16 * o, 16)], r1.at[pl.ds(48, 16)], 1, partner),
    ])
    acc[0:48] = gm[pl.ds(48 * s, 48)].astype(F32) + r1[0:48].astype(F32)
    acc[48:64] = sm[pl.ds(16 * s, 16)].astype(F32) + r1[48:64].astype(F32)
    snd2[...] = acc[...].astype(BF16)
    run([
        copy(snd2.at[pl.ds(8 * xk[k], 8)], r2.at[0, k], 2 + k, xs[k]) for k in range(3)
    ] + [
        copy(snd2.at[pl.ds(32 + 8 * yk[k], 8)], r2.at[1, k], 5 + k, ys[k]) for k in range(3)
    ])
    for part, at in ((0, 8 * x), (1, 32 + 8 * y)):
        acc2[pl.ds(8 * part, 8)] = (
            acc[pl.ds(at, 8)]
            + r2[part, 0].astype(F32)
            + r2[part, 1].astype(F32)
            + r2[part, 2].astype(F32)
        )
    snd3[...] = acc2[...].astype(BF16)
    run([
        copy(snd3.at[pl.ds(2 * yk[k], 2)], r3.at[0, k], 8 + k, ys[k]) for k in range(3)
    ] + [
        copy(snd3.at[pl.ds(8 + 2 * xk[k], 2)], r3.at[1, k], 11 + k, xs[k]) for k in range(3)
    ])
    for part, at in ((0, 2 * y), (1, 8 + 2 * x)):
        acc3[pl.ds(2 * part, 2)] = (
            acc2[pl.ds(at, 2)]
            + r3[part, 0].astype(F32)
            + r3[part, 1].astype(F32)
            + r3[part, 2].astype(F32)
        )
    snd4[...] = acc3[...].astype(BF16)
    zcopy = copier(z_send, z_recv)
    for k in range(7):
        owner = zk[k]

        @pl.when(lax.rem(owner, 2) == 0)
        def _():
            zcopy(snd4.at[owner // 2], r4.at[k], k, zs[k]).start()

    @pl.when(lax.rem(z, 2) == 0)
    def _():
        for k in range(7):
            zcopy(snd4.at[0], r4.at[k], k, zs[k]).wait_recv()
        total = acc3[z // 2]
        for k in range(7):
            total = total + r4[k].astype(F32)
        fin[...] = total.astype(BF16)
        res4[z // 2] = fin[...]
        for k in range(7):
            zcopy(fin, res4.at[z // 2], 7 + k, zs[k]).start()

    for k in range(7):
        owner = zk[k]

        @pl.when(lax.rem(owner, 2) == 0)
        def _():
            zcopy(snd4.at[owner // 2], r4.at[k], k, zs[k]).wait_send()
            zcopy(fin, res4.at[owner // 2], 7 + (6 - k), zs[k]).wait_recv()

    @pl.when(lax.rem(z, 2) == 0)
    def _():
        for k in range(7):
            zcopy(fin, res4.at[z // 2], 7 + k, zs[k]).wait_send()

    res3[pl.ds(2 * y, 2)] = res4[0:2]
    res3[pl.ds(8 + 2 * x, 2)] = res4[2:4]
    run([
        copy(res4.at[pl.ds(0, 2)], res3.at[pl.ds(2 * y, 2)], 14 + k, ys[k]) for k in range(3)
    ] + [
        copy(res4.at[pl.ds(2, 2)], res3.at[pl.ds(8 + 2 * x, 2)], 17 + k, xs[k]) for k in range(3)
    ])
    res2[pl.ds(8 * x, 8)] = res3[0:8]
    res2[pl.ds(32 + 8 * y, 8)] = res3[8:16]
    run([
        copy(res3.at[pl.ds(0, 8)], res2.at[pl.ds(8 * x, 8)], 20 + k, xs[k]) for k in range(3)
    ] + [
        copy(res3.at[pl.ds(8, 8)], res2.at[pl.ds(32 + 8 * y, 8)], 23 + k, ys[k]) for k in range(3)
    ])
    out_g[pl.ds(48 * s, 48)] = res2[0:48]
    out_s[pl.ds(16 * s, 16)] = res2[48:64]
    run([
        copy(res2.at[pl.ds(0, 48)], out_g.at[pl.ds(48 * s, 48)], 26, partner),
        copy(res2.at[pl.ds(48, 16)], out_s.at[pl.ds(16 * s, 16)], 27, partner),
    ])


def add_up(gm, sm):
    return pl.pallas_call(
        add_up_kernel,
        out_shape=(
            jax.ShapeDtypeStruct((96, 16, 384), BF16),
            jax.ShapeDtypeStruct((32, 16, 384), BF16),
        ),
        in_specs=[VM] * 2,
        out_specs=(VM,) * 2,
        scratch_shapes=[
            pltpu.VMEM((64, 16, 384), F32),
            pltpu.VMEM((64, 16, 384), BF16),
            pltpu.VMEM((16, 16, 384), BF16),
            pltpu.VMEM((4, 16, 384), BF16),
            pltpu.VMEM((16, 384), BF16),
            pltpu.VMEM((16, 16, 384), F32),
            pltpu.VMEM((4, 16, 384), F32),
            pltpu.VMEM((64, 16, 384), BF16),
            pltpu.VMEM((2, 3, 8, 16, 384), BF16),
            pltpu.VMEM((2, 3, 2, 16, 384), BF16),
            pltpu.VMEM((7, 16, 384), BF16),
            pltpu.VMEM((64, 16, 384), BF16),
            pltpu.VMEM((16, 16, 384), BF16),
            pltpu.VMEM((4, 16, 384), BF16),
            pltpu.SemaphoreType.DMA((28,)),
            pltpu.SemaphoreType.DMA((28,)),
            pltpu.SemaphoreType.DMA((14,)),
            pltpu.SemaphoreType.DMA((14,)),
        ],
        compiler_params=pltpu.CompilerParams(
            collective_id=3, has_side_effects=True, vmem_limit_bytes=LIMIT
        ),
        name="add_up",
    )(gm, sm)


def local(tokens, ln_gain, w_query, w_keyval, w_out, w_merge, owner_map, relay_grad):
    gain = ln_gain.reshape(1, C)
    own_tok, region, rims, corners, mg, owners = intake(tokens[0], relay_grad[0], owner_map)
    merged, gm, go, qg, og, kv_main, kv_d, kv_h, kv_c = compute(
        own_tok, region, rims, corners, mg, gain, w_query, w_keyval, w_out, w_merge
    )
    r_main, r_d, r_h, r_c, r_merged = exchange(kv_main, kv_d, kv_h, kv_c, merged)
    token_grad, relayed, small = finish(
        own_tok, qg, og, r_main, r_d, r_h, r_c, merged, r_merged, owners, gain, w_query,
        w_keyval, go,
    )
    big, rest = add_up(gm.reshape(96, 16, 384), small.reshape(32, 16, 384))
    scale = (2.0 * 128000) ** (-0.5)
    rest = rest.reshape(512, 384)
    scaled = lambda a: a.astype(F32) * scale
    return (
        relayed[None],
        token_grad[None],
        scaled(rest[384, :C]),
        scaled(rest[192:384, :C]),
        scaled(rest[:192]),
        scaled(rest[192:384, C:]),
        scaled(big.reshape(1536, 384)),
    )


def solution(mesh):
    rows = P("stream", ("depth", "height"), None)
    cells = P("stream", "depth", "height", None)
    return jax.shard_map(
        local,
        mesh=mesh,
        in_specs=(cells, P(), P(), P(), P(), P(), P("depth", "height"), rows),
        out_specs=(rows, cells, P(), P(), P(), P(), P()),
        check_vma=False,
    )
```

```python
import functools

import jax
import jax.numpy as jnp
import numpy as np
from jax import lax
from jax.experimental import pallas as pl
from jax.experimental.pallas import tpu as pltpu
from jax.sharding import PartitionSpec as P

C = 192
HEADS = 6
EPS = 1e-05
N_DEPTH = 4
N_HEIGHT = 32
SCALE = 32 ** (-0.5)
EXP2_SCALE = SCALE * 1.4426950408889634
MESH = pl.DeviceIdType.MESH
F32 = jnp.float32
BF16 = jnp.bfloat16
VM = pl.BlockSpec(memory_space=pltpu.VMEM)
SM = pl.BlockSpec(memory_space=pltpu.SMEM)
LIMIT = 60 * 1024 * 1024


def dot(a, b):
    return lax.dot_general(a, b, (((1,), (0,)), ((), ())), preferred_element_type=F32)


def dot_nt(a, b):
    return lax.dot_general(a, b, (((1,), (1,)), ((), ())), preferred_element_type=F32)


def dot_tn(a, b):
    return lax.dot_general(a, b, (((0,), (0,)), ((), ())), preferred_element_type=F32)


def place():
    return lax.axis_index("stream"), lax.axis_index("depth"), lax.axis_index("height")


def neighbours():
    s, d, h = place()
    dl, dh = lax.rem(d + N_DEPTH - 1, N_DEPTH), lax.rem(d + 1, N_DEPTH)
    hl, hh = lax.rem(h + N_HEIGHT - 1, N_HEIGHT), lax.rem(h + 1, N_HEIGHT)
    o = 1 - s
    return {
        "p": (o, d, h),
        "dl": (o, dl, h),
        "dh": (o, dh, h),
        "hl": (o, d, hl),
        "hh": (o, d, hh),
        "ll": (o, dl, hl),
        "lh": (o, dl, hh),
        "hdl": (o, dh, hl),
        "hdh": (o, dh, hh),
        "sl": (s, d, hl),
        "sh": (s, d, hh),
    }


def greet(peers):
    barrier = pltpu.get_barrier_semaphore()
    for peer in peers:
        pl.semaphore_signal(barrier, inc=1, device_id=peer, device_id_type=MESH)
    pl.semaphore_wait(barrier, len(peers))


def copier(send_sem, recv_sem):
    def make(src, dst, index, peer):
        return pltpu.make_async_remote_copy(
            src_ref=src,
            dst_ref=dst,
            send_sem=send_sem.at[index],
            recv_sem=recv_sem.at[index],
            device_id=peer,
            device_id_type=MESH,
        )

    return make


def relay_ranks(fl, fs, fr):
    _, _, h = place()
    left, right = lax.rem(h + N_HEIGHT - 1, N_HEIGHT), lax.rem(h + 1, N_HEIGHT)

    def before(a, b):
        return jnp.where(a < b, 1, 0)

    rank_l = fs * before(h, left) + fr * before(right, left)
    rank_s = fl * before(left, h) + fr * before(right, h)
    rank_r = fl * before(left, right) + fs * before(h, right)
    return rank_l, rank_s, rank_r


def wide(row):
    return jnp.concatenate([row, row, row], axis=1)


def normalized(x):
    centre = jnp.mean(x, -1, keepdims=True)
    shifted = x - centre
    inverse = lax.rsqrt(jnp.mean(shifted * shifted, -1, keepdims=True) + EPS)
    return shifted * inverse, inverse


def eight_index(window, q):
    wi, di, hi = window // 4, (window // 2) % 2, window % 2
    a = (q * 41) >> 10
    rest = q - a * 25
    b = (rest * 205) >> 10
    c = rest - b * 5
    w, d, h = a + 5 * wi, b + 5 * di, c + 5 * hi
    offset = ((d & 1) * 2 + (h & 1)) * 2 + (w & 1)
    cell = ((d >> 1) * 5 + (h >> 1)) * 5 + (w >> 1)
    return jnp.where(q < 125, offset * 128 + cell, -1)


def lane_row(tile):
    return jnp.concatenate([tile[j : j + 1] for j in range(15)], axis=1)


class Adder:
    def __init__(self, refs, send_sem, recv_sem):
        (self.src, self.out, self.r1, self.acc, self.snd2, self.r2a, self.r2b, self.acc2,
         self.snd3, self.r3a, self.r3b, self.r4, self.res4, self.res3, self.res2) = refs
        self.copy = copier(send_sem, recv_sem)
        s, d, h = place()
        zh, xy = h // 16, lax.rem(h, 16)
        x, y = xy // 4, lax.rem(xy, 4)
        self.s, self.x, self.y, self.z = s, x, y, zh * 4 + d
        self.partner = (1 - s, d, h)
        self.xk = [lax.rem(x + k, 4) for k in (1, 2, 3)]
        self.yk = [lax.rem(y + k, 4) for k in (1, 2, 3)]
        self.xs = [(s, d, zh * 16 + t * 4 + y) for t in self.xk]
        self.ys = [(s, d, zh * 16 + x * 4 + t) for t in self.yk]
        zk = [lax.rem(self.z + k, 8) for k in range(1, 8)]
        self.zk = zk
        self.zs = [(s, lax.rem(t, 4), (t // 4) * 16 + xy) for t in zk]

    def copies(self, step):
        c, x, y, z = self.copy, self.x, self.y, self.z
        three = range(3)
        if step == 1:
            return [c(self.src.at[1 - self.s], self.r1, 0, self.partner)]
        if step == 2:
            return [
                c(self.snd2.at[pl.ds(8 * self.xk[k], 8)], self.r2a.at[k], 1 + k, self.xs[k])
                for k in three
            ] + [
                c(self.snd2.at[pl.ds(32 + 4 * self.yk[k], 4)], self.r2b.at[k], 4 + k, self.ys[k])
                for k in three
            ]
        if step == 3:
            return [
                c(self.snd3.at[pl.ds(2 * self.yk[k], 2)], self.r3a.at[k], 7 + k, self.ys[k])
                for k in three
            ] + [
                c(self.snd3.at[8 + self.xk[k]], self.r3b.at[k], 10 + k, self.xs[k])
                for k in three
            ]
        if step == 4:
            return [c(self.r4.at[z], self.r4.at[z], 13 + k, self.zs[k]) for k in range(7)]
        if step == 5:
            return [
                c(self.res4.at[pl.ds(0, 2)], self.res3.at[pl.ds(2 * y, 2)], 20 + k, self.ys[k])
                for k in three
            ] + [c(self.res4.at[2], self.res3.at[8 + x], 23 + k, self.xs[k]) for k in three]
        if step == 6:
            return [
                c(self.res3.at[pl.ds(0, 8)], self.res2.at[pl.ds(8 * x, 8)], 26 + k, self.xs[k])
                for k in three
            ] + [
                c(self.res3.at[pl.ds(8, 4)], self.res2.at[pl.ds(32 + 4 * y, 4)], 29 + k, self.ys[k])
                for k in three
            ]
        return [c(self.res2, self.out.at[self.s], 32, self.partner)]

    def start(self, step):
        for one in self.copies(step):
            one.start()

    def finish(self, step):
        for one in self.copies(step):
            one.wait()
        x, y, z = self.x, self.y, self.z

        def total(first, parts):
            for part in parts:
                first = first + part.astype(F32)
            return first

        if step == 1:
            self.acc[...] = self.src[self.s].astype(F32) + self.r1[...].astype(F32)
            self.snd2[...] = self.acc[...].astype(BF16)
        elif step == 2:
            ra, rb = self.r2a, self.r2b
            self.acc2[0:8] = total(self.acc[pl.ds(8 * x, 8)], [ra[0], ra[1], ra[2]])
            self.acc2[8:12] = total(self.acc[pl.ds(32 + 4 * y, 4)], [rb[0], rb[1], rb[2]])
            self.snd3[...] = self.acc2[...].astype(BF16)
        elif step == 3:
            ra, rb = self.r3a, self.r3b
            self.r4[z, 0:2] = total(self.acc2[pl.ds(2 * y, 2)], [ra[0], ra[1], ra[2]]).astype(BF16)
            self.r4[z, 2] = total(self.acc2[8 + x], [rb[0], rb[1], rb[2]]).astype(BF16)
        elif step == 4:
            done = total(self.r4[0].astype(F32), [self.r4[k] for k in range(1, 8)]).astype(BF16)
            self.res4[...] = done
            self.res3[pl.ds(2 * y, 2)] = done[0:2]
            self.res3[8 + x] = done[2]
        elif step == 5:
            self.res2[pl.ds(8 * x, 8)] = self.res3[0:8]
            self.res2[pl.ds(32 + 4 * y, 4)] = self.res3[8:12]
        elif step == 6:
            self.out[self.s] = self.res2[...]

    def advance(self, step):
        self.finish(step)
        self.start(step + 1)


def adder_scratch(lanes, with_src):
    def of(*dims, kind=BF16):
        return pltpu.VMEM((*dims, 16, lanes), kind)

    return [of(2, 48)] * with_src + [
        of(48),
        of(48, kind=F32),
        of(48),
        of(3, 8),
        of(3, 4),
        of(12, kind=F32),
        of(12),
        of(3, 2),
        of(3),
        of(8, 3),
        of(3),
        of(12),
        of(48),
    ]


N_ADDER = 13


def whole_kernel(
    tok, rg, own, gain, wq, wkv, wo, wm, g, gt,
    token_grad, relayed, out_g, out_s,
    *scratch,
):
    (stage, own_tok, region, hstage, hsend, rims, cst, csend, corners, rimst, rimx,
     rows, mg_send, mg_recv, mg, own_send, owners,
     qreg, xreg, kreg, vreg, nreg, norm_n, inv_n, acck, accv, wk, wv,
     abuf, cts, qs, og_e, out_w, pt, qbd, qbd_t, cgbd, cgbd_t, ctx_t, qg_t, go, og_n,
     merged, r_merged, kv_h, r_h, kv_c, cstage, r_c, kv_main, r_main, kv_d, r_d,
     normals, kvs, qgs, stage2, wins, wide_out,
     send_sem, recv_sem, g_send, g_recv, s_send, s_recv) = scratch[:65]
    rest = scratch[65:]
    qg_n = qreg
    big = Adder((rest[0], out_g, *rest[1 : 1 + N_ADDER]), g_send, g_recv)
    rest = rest[1 + N_ADDER :]
    small = Adder((rest[0], out_s, *rest[1 : 1 + N_ADDER]), s_send, s_recv)
    s, dep, hei = place()
    peers = neighbours()
    copy = copier(send_sem, recv_sem)
    greeted = list(peers.values()) + big.xs + big.ys + big.zs
    barrier = pltpu.get_barrier_semaphore()
    for peer in greeted:
        pl.semaphore_signal(barrier, inc=1, device_id=peer, device_id_type=MESH)

    own_send[...] = jnp.full((8, 128), own[0, 0], jnp.int32)
    owners[1] = own_send[...]
    stage[...] = jnp.zeros_like(stage)
    hstage[...] = jnp.zeros_like(hstage)
    cst[...] = jnp.zeros_like(cst)
    for d in range(10):
        x = tok[d].astype(F32)
        stage[d, 1:7, :] = x[0:6]
        stage[d, 9:14, :] = x[5:10]
        stage[d, 8:9, :] = x[4:5]
        hstage[0, d : d + 1, :] = x[0:1]
        hstage[1, d : d + 1, :] = x[9:10]
        if d in (0, 9):
            for side in range(2):
                r = x[9 * side : 9 * side + 1]
                for j in range(15):
                    cst[2 * (d // 9) + side, j : j + 1, :] = r[:, 128 * j : 128 * j + 128]
    own_tok[...] = stage[...].astype(BF16)
    hsend[...] = hstage[...].astype(BF16)
    csend[...] = cst[...].astype(BF16)

    gains = gain[...]
    for pair in range(5):
        lanes = slice(384 * pair, 384 * pair + 384)
        own2 = stage[:, :, lanes].reshape(160, 384)
        for half in range(2):
            w = 2 * pair + half
            x = own2[:, 192 * half : 192 * half + 192]
            normed, inverse = normalized(x)
            norm_n[w] = normed
            inv_n[w] = inverse
            qreg[w] = dot((normed * gains).astype(BF16), wq[...]).reshape(10, 16, C)
            xreg[w] = x.reshape(10, 16, C)
    pl.semaphore_wait(barrier, len(greeted))
    to_left = copy(own_send, owners.at[2], 0, peers["sl"])
    to_right = copy(own_send, owners.at[0], 1, peers["sh"])
    far = [
        copy(hsend.at[1], rims.at[0], 5, peers["hh"]),
        copy(hsend.at[0], rims.at[1], 6, peers["hl"]),
        copy(csend.at[3], corners.at[0], 7, peers["hdh"]),
        copy(csend.at[2], corners.at[1], 8, peers["hdl"]),
        copy(csend.at[1], corners.at[2], 9, peers["lh"]),
        copy(csend.at[0], corners.at[3], 10, peers["ll"]),
    ]
    near = [
        copy(own_tok, region.at[pl.ds(1, 10)], 2, peers["p"]),
        copy(own_tok.at[9], region.at[0], 3, peers["dh"]),
        copy(own_tok.at[0], region.at[11], 4, peers["dl"]),
    ]
    to_left.start()
    to_right.start()
    for one in far + near:
        one.start()

    rows[...] = jnp.zeros_like(rows)

    def spread(i, carry):
        x = rg[:, pl.ds(pl.multiple_of(i * 384, 128), 384)].astype(F32)
        for k in range(3):
            rows[k, pl.ds(i, 1), :] = x[k : k + 1]
        return carry

    lax.fori_loop(0, 125, spread, 0)
    acck[...] = jnp.zeros_like(acck)
    accv[...] = jnp.zeros_like(accv)
    qbd_t[...] = jnp.zeros_like(qbd_t)
    cgbd_t[...] = jnp.zeros_like(cgbd_t)
    ones = lax.broadcasted_iota(jnp.int32, (64, 768), 0)
    qbd_t[192:256, :] = jnp.where(ones == 0, 1.0, 0.0).astype(BF16)
    go[...] = jnp.zeros_like(go)
    wk[...] = jnp.zeros_like(wk)
    wk[:, :C] = wkv[:, :C]
    wv[...] = wkv[:, C:]

    row = lax.broadcasted_iota(jnp.int32, (192, 256), 0)
    lane = lax.broadcasted_iota(jnp.int32, (192, 256), 1)
    rd, rs = row >> 4, row & 15
    off_depth = ((rd == 0) & (dep == 0)) | ((rd == 11) & (dep == N_DEPTH - 1))
    bias = jnp.where((off_depth | ((rs & 7) == 7)) & (lane == 192), -1e30, 0.0)
    edge = jnp.where(lane == 192, -1e30, 0.0).reshape(12, 16, 256)
    for w in (0, 11):
        kreg[w] = edge
        vreg[w] = jnp.zeros((12, 16, C), F32)

    for one in near:
        one.wait()
    for pair in range(5):
        lanes = slice(384 * pair, 384 * pair + 384)
        reg2 = region[:, :, lanes].astype(F32).reshape(192, 384)
        for half in range(2):
            w = 2 * pair + half
            y = reg2[:, 192 * half : 192 * half + 192]
            normed, _ = normalized(y)
            normal = (normed * gains).astype(BF16)
            nreg[w] = normed.reshape(12, 16, C)
            kreg[w + 1] = (dot(normal, wk[...]) + bias).reshape(12, 16, 256)
            vreg[w + 1] = dot(normal, wv[...]).reshape(12, 16, C)
    for one in far:
        one.wait()
    rimst[...] = jnp.zeros_like(rimst)
    for side in range(2):
        rimst[side, 1:11, :] = rims[side].astype(F32)[0:10]
        rimst[side, 0:1, :] = lane_row(corners[side].astype(F32))
        rimst[side, 11:12, :] = lane_row(corners[2 + side].astype(F32))
        for pair in range(5):
            x = rimst[side, :, 384 * pair : 384 * pair + 384]
            rimx[side, 2 * pair] = x[:, :C]
            rimx[side, 2 * pair + 1] = x[:, C:]
    rlane = lax.broadcasted_iota(jnp.int32, (160, 256), 1)
    rrow = lax.broadcasted_iota(jnp.int32, (160, 256), 0) & 15
    off_depth = ((rrow == 0) & (dep == 0)) | ((rrow == 11) & (dep == N_DEPTH - 1))
    for side in range(2):
        off = off_depth | (hei == (N_HEIGHT - 1) * side)
        rbias = jnp.where(off & (rlane == 192), -1e30, 0.0)
        normed, _ = normalized(rimx[side].reshape(160, C))
        normal = (normed * gains).astype(BF16)
        kr = (dot(normal, wk[...]) + rbias).reshape(10, 16, 256)
        vr = dot(normal, wv[...]).reshape(10, 16, C)
        nr = normed.reshape(10, 16, C)
        at = slice(14 * side, 14 * side + 1)
        for w in range(10):
            for d in range(12):
                kreg[w + 1, d, at, :] = kr[w, d : d + 1]
                vreg[w + 1, d, at, :] = vr[w, d : d + 1]
                nreg[w, d, at, :] = nr[w, d : d + 1]

    to_left.wait()
    to_right.wait()
    fl = jnp.where(owners[0, 0:1, :] == hei, 1, 0)
    fs = jnp.where(owners[1, 0:1, :] == hei, 1, 0)
    fr = jnp.where(owners[2, 0:1, :] == hei, 1, 0)
    rank_l, rank_s, rank_r = relay_ranks(fl, fs, fr)

    def pick_row(rank):
        rank = wide(rank)
        return jnp.where(rank == 0, rows[0], jnp.where(rank == 1, rows[1], rows[2]))

    mg_send[0] = pick_row(rank_l).astype(BF16)
    mg_send[1] = pick_row(rank_r).astype(BF16)
    back = [
        copy(mg_send.at[0], mg_recv.at[1], 11, peers["sl"]),
        copy(mg_send.at[1], mg_recv.at[0], 12, peers["sh"]),
    ]
    for one in back:
        one.start()

    def window_of(i, first):
        hi = (i // 4 + first) % 2
        di, wi = i % 2, (i // 2) % 2
        hs = pl.ds(pl.multiple_of(hi * 8, 8), 8)
        cells = (pl.ds(wi * 5, 5), pl.ds(di * 5, 5), hs, slice(None))
        around = (pl.ds(wi * 5, 7), pl.ds(di * 5, 7), hs, slice(None))
        return wi * 4 + di * 2 + hi, cells, around

    head = lax.broadcasted_iota(jnp.int32, (128, C), 1) >> 5
    odd = hei % 2

    def forward(i, carry):
        n, cells, around = window_of(i, 1 - odd)
        q_w = dot(gt[...], qreg[cells].reshape(200, C).astype(BF16))
        x_w = dot(gt[...], xreg[cells].reshape(200, C).astype(BF16))
        q = lax.broadcasted_iota(jnp.int32, (1024, 128), 1)
        col = lax.broadcasted_iota(jnp.int32, (1024, 128), 0)
        pt[n] = jnp.where(eight_index(n, q) == col, 1.0, 0.0).astype(BF16)
        qs[n] = q_w.astype(BF16)
        q_t = q_w.T.astype(BF16)
        for m in range(HEADS):
            r, l = slice(32 * m, 32 * m + 32), slice(128 * m, 128 * m + 128)
            qbd_t[r, l] = q_t[r]
        k = kreg[around].reshape(392, 256).astype(BF16)
        v_t = vreg[around].reshape(392, C).T.astype(BF16)
        for p in range(3):
            l = slice(256 * p, 256 * p + 256)
            e = jnp.exp2(dot(k, qbd_t[:, l]) * EXP2_SCALE)
            a = (e * (1.0 / jnp.sum(e, 0, keepdims=True))).astype(BF16)
            abuf[n, :, l] = a
            c = dot(v_t[64 * p : 64 * p + 64], a)
            ctx_t[64 * p : 64 * p + 32, :] = c[:32, :128]
            ctx_t[64 * p + 32 : 64 * p + 64, :] = c[32:, 128:]
        c_t = ctx_t[...]
        cts[n] = c_t.astype(BF16)
        out_w[n] = (dot(c_t.T.astype(BF16), wo[...]) + x_w).astype(BF16)
        return carry

    lax.fori_loop(0, 8, forward, 0)
    out_e = dot(pt[0], out_w[0])
    for i in range(1, 8):
        out_e = out_e + dot(pt[i], out_w[i])
    out_b = out_e.astype(BF16)
    total = jnp.zeros((128, 384), F32)
    for o in range(8):
        total = total + dot(out_b[128 * o : 128 * o + 128], wm[192 * o : 192 * o + 192, :])
    merged[...] = total.astype(BF16)
    relays = [
        copy(merged, r_merged.at[1], 13, peers["sl"]),
        copy(merged, r_merged.at[0], 14, peers["sh"]),
    ]
    for one in relays:
        one.start()
    left, right = lax.rem(hei + N_HEIGHT - 1, N_HEIGHT), lax.rem(hei + 1, N_HEIGHT)
    target = wide(owners[1, 0:1, :])
    mine = pick_row(rank_s)
    for one in back:
        one.wait()
    mg[...] = jnp.where(
        target == left,
        mg_recv[0].astype(F32),
        jnp.where(target == right, mg_recv[1].astype(F32), mine),
    ).astype(BF16)
    for o in range(8):
        part = dot_tn(out_b[128 * o : 128 * o + 128], mg[...]).astype(BF16)
        big.src[o // 4, 12 * (o % 4) : 12 * (o % 4) + 12] = part.reshape(12, 16, 384)
    big.start(1)
    for o in range(8):
        og_e[128 * o : 128 * o + 128, :] = dot_nt(
            mg[...], wm[192 * o : 192 * o + 192, :]
        ).astype(BF16)

    cstage[...] = jnp.zeros_like(cstage)
    srow = lax.broadcasted_iota(jnp.int32, (16, 192), 0)
    scol = lax.broadcasted_iota(jnp.int32, (16, 192), 1)

    def rim_copies(side):
        hn = lax.rem(hei + 2 * side + N_HEIGHT - 1, N_HEIGHT)
        dl, dh = lax.rem(dep + N_DEPTH - 1, N_DEPTH), lax.rem(dep + 1, N_DEPTH)
        return [
            copy(kv_h.at[side], r_h.at[1 - side], 15 + side, (1 - s, dep, hn)),
            copy(kv_c.at[side], r_c.at[3 - side], 17 + side, (1 - s, dl, hn)),
            copy(kv_c.at[2 + side], r_c.at[1 - side], 19 + side, (1 - s, dh, hn)),
        ]

    def send_rim(side):
        pick = jnp.where(scol == srow * 16 + 14 * side, 1.0, 0.0).astype(BF16)
        for w in range(10):
            t = jnp.concatenate([acck[w + 1], accv[w + 1]], axis=-1)
            r = dot(pick, t.reshape(192, 384).astype(BF16))
            kv_h[side, w] = r.astype(BF16)
            cstage[0, w : w + 1, :] = r[0:1]
            cstage[1, w : w + 1, :] = r[11:12]
        kv_c[side] = cstage[0].astype(BF16)
        kv_c[2 + side] = cstage[1].astype(BF16)
        for one in rim_copies(side):
            one.start()

    def backward(i, carry):
        n, cells, around = window_of(i, odd)
        q = lax.broadcasted_iota(jnp.int32, (128, 1024), 0)
        col = lax.broadcasted_iota(jnp.int32, (128, 1024), 1)
        pick = jnp.where(eight_index(n, q) == col, 1.0, 0.0).astype(BF16)
        og_b = dot(pick, og_e[...]).astype(BF16)
        cg_w = dot_nt(og_b, wo[...]).astype(BF16).astype(F32)
        q_w = qs[n].astype(F32)
        cg_t = cg_w.T.astype(BF16)
        for m in range(HEADS):
            r, l = slice(32 * m, 32 * m + 32), slice(128 * m, 128 * m + 128)
            cgbd_t[r, l] = cg_t[r]
            qbd[l, :] = jnp.where(head == m, q_w, 0.0).astype(BF16)
            cgbd[l, :] = jnp.where(head == m, cg_w, 0.0).astype(BF16)
        k_t = kreg[around].reshape(392, 256)[:, :C].T.astype(BF16)
        v = vreg[around].reshape(392, C).astype(BF16)
        kg = jnp.zeros((392, C), F32)
        vg = jnp.zeros((392, C), F32)
        for p in range(3):
            l = slice(256 * p, 256 * p + 256)
            a = abuf[n, :, l]
            af = a.astype(F32)
            wg = dot(v, cgbd_t[:, l])
            mean = jnp.sum(wg * af, 0, keepdims=True)
            sg = (af * (wg - mean) * SCALE).astype(BF16)
            vg = vg + dot(a, cgbd[l, :])
            kg = kg + dot(sg, qbd[l, :])
            c = dot(k_t[64 * p : 64 * p + 64], sg)
            qg_t[64 * p : 64 * p + 32, :] = c[:32, :128]
            qg_t[64 * p + 32 : 64 * p + 64, :] = c[32:, 128:]
        acck[around] += kg.reshape(7, 7, 8, C)
        accv[around] += vg.reshape(7, 7, 8, C)
        go[...] += dot(cts[n], og_b)
        qg_w = qg_t[...].T.astype(BF16)
        qg_n[cells] = dot(g[...], qg_w).reshape(5, 5, 8, C)
        og_n[cells] = dot(g[...], og_b).reshape(5, 5, 8, C)
        for at, step in ((0, 1), (1, 2), (2, 3), (4, 4), (5, 5), (6, 6)):
            pl.when(i == at)(functools.partial(big.advance, step))
        pl.when(i == 3)(functools.partial(send_rim, odd))
        return carry

    lax.fori_loop(0, 8, backward, 0)

    send_rim(1 - odd)
    slot = lax.broadcasted_iota(jnp.int32, (12, 16, 384), 1)
    inner = (slot & 7 >= 1) & (slot & 7 <= 5)
    for w in range(10):
        t = jnp.concatenate([acck[w + 1], accv[w + 1]], axis=-1)
        kvs[192 * w : 192 * w + 192, :] = t.reshape(192, 384).astype(BF16)
        t = t + jnp.where(slot == 5, t[:, 8:9, :], jnp.where(slot == 9, t[:, 6:7, :], 0.0))
        b = jnp.where(inner, t, 0.0).astype(BF16)
        kv_main[w] = b[1:11]
        kv_d[0, w] = b[0]
        kv_d[1, w] = b[11]
    grads = [
        copy(kv_d.at[0], r_d.at[1], 21, peers["dl"]),
        copy(kv_d.at[1], r_d.at[0], 22, peers["dh"]),
        copy(kv_main, r_main, 23, peers["p"]),
    ]
    for one in grads:
        one.start()

    gain_sum = jnp.zeros((1, C), F32)
    for w in range(10):
        normed = nreg[w].reshape(192, C)
        normals[192 * w : 192 * w + 192, :] = (normed * gains).astype(BF16)
        ng = dot_nt(kvs[192 * w : 192 * w + 192, :], wkv[...])
        gain_sum = gain_sum + jnp.sum(ng * normed, 0, keepdims=True)
    part = dot_tn(normals[...], kvs[...]).astype(BF16)
    for j in range(3):
        small.src[0, 12 * j : 12 * j + 12] = part[:, 128 * j : 128 * j + 128].reshape(12, 16, 128)
    for w in range(10):
        normed = norm_n[w]
        normals[160 * w : 160 * w + 160, :] = (normed * gains).astype(BF16)
        qgs[160 * w : 160 * w + 160, :] = qg_n[w].reshape(160, C).astype(BF16)
        ng = dot_nt(qgs[160 * w : 160 * w + 160, :], wq[...])
        xreg[w] = ng.reshape(10, 16, C)
        gain_sum = gain_sum + jnp.sum(ng * normed, 0, keepdims=True)
    part = jnp.concatenate([dot_tn(normals[0:1600, :], qgs[...]), go[...]], axis=1).astype(BF16)
    for j in range(3):
        small.src[1, 12 * j : 12 * j + 12] = part[:, 128 * j : 128 * j + 128].reshape(12, 16, 128)
    first = lax.broadcasted_iota(jnp.int32, (16, 128), 0)
    tail = jnp.concatenate([gain_sum[:, 128:], jnp.zeros((1, 64), F32)], axis=1)
    small.src[:, 36:48] = jnp.zeros((2, 12, 16, 128), BF16)
    small.src[0, 36] = jnp.where(
        first == 0, gain_sum[:, :128], jnp.where(first == 1, tail, 0.0)
    ).astype(BF16)
    small.start(1)

    for one in relays:
        one.wait()
    parts = []
    for flag, rank, win in zip(
        (fl, fs, fr), (rank_l, rank_s, rank_r), (r_merged[0], merged[...], r_merged[1])
    ):
        parts.append((wide(jnp.where(flag == 1, rank, -1)), win.astype(F32)))
    for k in range(3):
        total = jnp.zeros((128, 384), F32)
        for key, win in parts:
            total = jnp.where(key == k, win, total)
        wins[k] = total
    small.advance(1)

    def lay(i, carry):
        lanes = pl.ds(pl.multiple_of(i * 384, 128), 384)
        for k in range(3):
            wide_out[k : k + 1, lanes] = wins[k, pl.ds(i, 1), :]
        return carry

    lax.fori_loop(0, 125, lay, 0)
    relayed[...] = wide_out[...].astype(BF16)
    small.advance(2)
    for one in grads + rim_copies(0) + rim_copies(1):
        one.wait()

    sl = lax.broadcasted_iota(jnp.int32, (16, 384), 0)
    for pair in range(5):
        lanes = slice(384 * pair, 384 * pair + 384)
        found = []
        for half in range(2):
            w = 2 * pair + half
            lo, hi = r_h[0, w].astype(F32), r_h[1, w].astype(F32)
            planes = []
            for d in range(10):
                lo_d, hi_d = lo[d + 1 : d + 2], hi[d + 1 : d + 2]
                if d in (0, 9):
                    e = 2 * (d // 9)
                    lo_d = lo_d + r_c[e].astype(F32)[w : w + 1]
                    hi_d = hi_d + r_c[e + 1].astype(F32)[w : w + 1]
                t = r_main[w, d].astype(F32)
                t = t + jnp.where(sl == 1, lo_d, jnp.where(sl == 13, hi_d, 0.0))
                if d in (0, 9):
                    t = t + r_d[d // 9, w].astype(F32)
                planes.append(t.astype(BF16))
            kv_b = jnp.concatenate(planes, axis=0)
            normed, inverse = norm_n[w], inv_n[w]
            u = (xreg[w].reshape(160, C) + dot_nt(kv_b, wkv[...])) * gains
            found.append(
                inverse
                * (
                    u
                    - jnp.mean(u, -1, keepdims=True)
                    - normed * jnp.mean(u * normed, -1, keepdims=True)
                )
                + og_n[w].reshape(160, C)
            )
        stage[:, :, lanes] = jnp.concatenate(found, axis=1).reshape(10, 16, 384)
        if pair in (0, 1, 3, 4):
            small.advance({0: 3, 1: 4, 3: 5, 4: 6}[pair])
    for d in range(10):
        x = stage[d]
        stage2[d, 0:5, :] = x[1:6]
        stage2[d, 5:10, :] = x[9:14]
    token_grad[...] = stage2[...].astype(BF16)
    small.finish(7)
    big.finish(7)


def whole(tok, rg, own, gain, wq, wkv, wo, wm):
    g = np.zeros((200, 128), np.float32)
    for a in range(5):
        for b in range(5):
            for c in range(5):
                g[(a * 5 + b) * 8 + c + 1, a * 25 + b * 5 + c] = 1
    g = jnp.asarray(g, BF16)
    vm, dma = pltpu.VMEM, pltpu.SemaphoreType.DMA
    scratch = [
        vm((10, 16, 1920), F32),
        vm((10, 16, 1920), BF16),
        vm((12, 16, 1920), BF16),
        vm((2, 16, 1920), F32),
        vm((2, 16, 1920), BF16),
        vm((2, 16, 1920), BF16),
        vm((4, 16, 128), F32),
        vm((4, 16, 128), BF16),
        vm((4, 16, 128), BF16),
        vm((2, 16, 1920), F32),
        vm((2, 10, 16, C), F32),
        vm((3, 128, 384), F32),
        vm((2, 128, 384), BF16),
        vm((2, 128, 384), BF16),
        vm((128, 384), BF16),
        vm((8, 128), jnp.int32),
        vm((3, 8, 128), jnp.int32),
        vm((10, 10, 16, C), F32),
        vm((10, 10, 16, C), F32),
        vm((12, 12, 16, 256), F32),
        vm((12, 12, 16, C), F32),
        vm((10, 12, 16, C), F32),
        vm((10, 160, C), F32),
        vm((10, 160, 1), F32),
        vm((12, 12, 16, C), F32),
        vm((12, 12, 16, C), F32),
        vm((C, 256), BF16),
        vm((C, C), BF16),
        vm((8, 392, 768), BF16),
        vm((8, C, 128), BF16),
        vm((8, 128, C), BF16),
        vm((1024, C), BF16),
        vm((8, 128, C), BF16),
        vm((8, 1024, 128), BF16),
        vm((768, C), BF16),
        vm((256, 768), BF16),
        vm((768, C), BF16),
        vm((C, 768), BF16),
        vm((C, 128), F32),
        vm((C, 128), F32),
        vm((C, C), F32),
        vm((10, 10, 16, C), F32),
        vm((128, 384), BF16),
        vm((2, 128, 384), BF16),
        vm((2, 10, 16, 384), BF16),
        vm((2, 10, 16, 384), BF16),
        vm((4, 16, 384), BF16),
        vm((2, 16, 384), F32),
        vm((4, 16, 384), BF16),
        vm((10, 10, 16, 384), BF16),
        vm((10, 10, 16, 384), BF16),
        vm((2, 10, 16, 384), BF16),
        vm((2, 10, 16, 384), BF16),
        vm((1920, C), BF16),
        vm((1920, 384), BF16),
        vm((1600, C), BF16),
        vm((10, 10, 1920), F32),
        vm((3, 128, 384), F32),
        vm((3, 48000), F32),
        dma((24,)), dma((24,)),
        dma((33,)), dma((33,)),
        dma((33,)), dma((33,)),
    ]
    scratch += adder_scratch(384, True) + adder_scratch(128, True)
    return pl.pallas_call(
        whole_kernel,
        out_shape=(
            jax.ShapeDtypeStruct((10, 10, 1920), BF16),
            jax.ShapeDtypeStruct((3, 48000), BF16),
            jax.ShapeDtypeStruct((2, 48, 16, 384), BF16),
            jax.ShapeDtypeStruct((2, 48, 16, 128), BF16),
        ),
        in_specs=[VM, VM, SM] + [VM] * 7,
        out_specs=(VM,) * 4,
        scratch_shapes=scratch,
        compiler_params=pltpu.CompilerParams(
            collective_id=1, has_side_effects=True, vmem_limit_bytes=LIMIT
        ),
        name="whole",
    )(tok, rg, own, gain, wq, wkv, wo, wm, g, g.T)


def local(tokens, ln_gain, w_query, w_keyval, w_out, w_merge, owner_map, relay_grad):
    token_grad, relayed, big, small = whole(
        tokens[0], relay_grad[0], owner_map, ln_gain.reshape(1, C), w_query, w_keyval, w_out,
        w_merge,
    )
    scale = (2.0 * 128000) ** (-0.5)
    scaled = lambda a: a.astype(F32) * scale

    def joined(half):
        tiles = small[half, :36].reshape(3, 12 * 16, 128)
        return jnp.concatenate([tiles[0], tiles[1], tiles[2]], axis=1)

    keyval, both = joined(0), joined(1)
    return (
        relayed[None],
        token_grad[None],
        scaled(small[0, 36, 0:2].reshape(256)[:C]),
        scaled(both[:, :C]),
        scaled(keyval),
        scaled(both[:, C:]),
        scaled(big.reshape(1536, 384)),
    )

def solution(mesh):
    rows = P("stream", ("depth", "height"), None)
    cells = P("stream", "depth", "height", None)
    return jax.shard_map(
        local,
        mesh=mesh,
        in_specs=(cells, P(), P(), P(), P(), P(), P("depth", "height"), rows),
        out_specs=(rows, cells, P(), P(), P(), P(), P()),
        check_vma=False,
    )
```

```python
import functools

import jax
import jax.numpy as jnp
import numpy as np
from jax import lax
from jax.experimental import pallas as pl
from jax.experimental.pallas import tpu as pltpu
from jax.sharding import PartitionSpec as P

C = 192
HEADS = 6
EPS = 1e-05
N_DEPTH = 4
N_HEIGHT = 32
SCALE = 32 ** (-0.5)
EXP2_SCALE = SCALE * 1.4426950408889634
MESH = pl.DeviceIdType.MESH
F32 = jnp.float32
BF16 = jnp.bfloat16
VM = pl.BlockSpec(memory_space=pltpu.VMEM)
SM = pl.BlockSpec(memory_space=pltpu.SMEM)
LIMIT = 62 * 1024 * 1024


def dot(a, b):
    return lax.dot_general(a, b, (((1,), (0,)), ((), ())), preferred_element_type=F32)


def dot_nt(a, b):
    return lax.dot_general(a, b, (((1,), (1,)), ((), ())), preferred_element_type=F32)


def dot_tn(a, b):
    return lax.dot_general(a, b, (((0,), (0,)), ((), ())), preferred_element_type=F32)


def place():
    return lax.axis_index("stream"), lax.axis_index("depth"), lax.axis_index("height")


def neighbours():
    s, d, h = place()
    dl, dh = lax.rem(d + N_DEPTH - 1, N_DEPTH), lax.rem(d + 1, N_DEPTH)
    hl, hh = lax.rem(h + N_HEIGHT - 1, N_HEIGHT), lax.rem(h + 1, N_HEIGHT)
    o = 1 - s
    return {
        "p": (o, d, h),
        "dl": (o, dl, h),
        "dh": (o, dh, h),
        "hl": (o, d, hl),
        "hh": (o, d, hh),
        "ll": (o, dl, hl),
        "lh": (o, dl, hh),
        "hdl": (o, dh, hl),
        "hdh": (o, dh, hh),
        "sl": (s, d, hl),
        "sh": (s, d, hh),
    }


def greet(peers):
    barrier = pltpu.get_barrier_semaphore()
    for peer in peers:
        pl.semaphore_signal(barrier, inc=1, device_id=peer, device_id_type=MESH)
    pl.semaphore_wait(barrier, len(peers))


def copier(send_sem, recv_sem):
    def make(src, dst, index, peer):
        return pltpu.make_async_remote_copy(
            src_ref=src,
            dst_ref=dst,
            send_sem=send_sem.at[index],
            recv_sem=recv_sem.at[index],
            device_id=peer,
            device_id_type=MESH,
        )

    return make


def relay_ranks(fl, fs, fr):
    _, _, h = place()
    left, right = lax.rem(h + N_HEIGHT - 1, N_HEIGHT), lax.rem(h + 1, N_HEIGHT)

    def before(a, b):
        return jnp.where(a < b, 1, 0)

    rank_l = fs * before(h, left) + fr * before(right, left)
    rank_s = fl * before(left, h) + fr * before(right, h)
    rank_r = fl * before(left, right) + fs * before(h, right)
    return rank_l, rank_s, rank_r


def wide(row):
    return jnp.concatenate([row, row, row], axis=1)


def normalized(x):
    centre = jnp.mean(x, -1, keepdims=True)
    shifted = x - centre
    inverse = lax.rsqrt(jnp.mean(shifted * shifted, -1, keepdims=True) + EPS)
    return shifted * inverse, inverse


def eight_index(window, q):
    wi, di, hi = window // 4, (window // 2) % 2, window % 2
    a = (q * 41) >> 10
    rest = q - a * 25
    b = (rest * 205) >> 10
    c = rest - b * 5
    w, d, h = a + 5 * wi, b + 5 * di, c + 5 * hi
    offset = ((d & 1) * 2 + (h & 1)) * 2 + (w & 1)
    cell = ((d >> 1) * 5 + (h >> 1)) * 5 + (w >> 1)
    return jnp.where(q < 125, offset * 128 + cell, -1)


def lane_row(tile):
    return jnp.concatenate([tile[j : j + 1] for j in range(15)], axis=1)


class Adder:
    def __init__(self, refs, send_sem, recv_sem):
        (self.src, self.out, self.r1, self.snd2, self.r2, self.r4, self.res4,
         self.res2) = refs
        self.copy = copier(send_sem, recv_sem)
        s, d, h = place()
        zh, xy = h // 16, lax.rem(h, 16)
        self.s, self.xy, self.z = s, xy, zh * 4 + d
        self.partner = (1 - s, d, h)
        self.pk = [lax.rem(xy + k, 16) for k in range(1, 16)]
        self.ps = [(s, d, zh * 16 + t) for t in self.pk]
        self.zs = []
        for k in range(1, 8):
            t = lax.rem(self.z + k, 8)
            self.zs.append((s, lax.rem(t, 4), (t // 4) * 16 + xy))

    def copies(self, step):
        c, xy, z = self.copy, self.xy, self.z
        if step == 1:
            return [c(self.src.at[1 - self.s], self.r1, 0, self.partner)]
        if step == 2:
            return [
                c(self.snd2.at[pl.ds(3 * self.pk[k], 3)], self.r2.at[k], 1 + k, self.ps[k])
                for k in range(15)
            ]
        if step == 3:
            return [c(self.r4.at[z], self.r4.at[z], 16 + k, self.zs[k]) for k in range(7)]
        if step == 4:
            at = pl.ds(3 * xy, 3)
            return [c(self.res4, self.res2.at[at], 23 + k, self.ps[k]) for k in range(15)]
        return [c(self.res2, self.out.at[self.s], 38, self.partner)]

    def start(self, step):
        for one in self.copies(step):
            one.start()

    def finish(self, step):
        for one in self.copies(step):
            one.wait()
        xy, z = self.xy, self.z
        if step == 1:
            total = self.src[self.s].astype(F32) + self.r1[...].astype(F32)
            self.snd2[...] = total.astype(BF16)
        elif step == 2:
            at = pl.ds(3 * xy, 3)
            total = self.src[self.s, at].astype(F32) + self.r1[at].astype(F32)
            for k in range(15):
                total = total + self.r2[k].astype(F32)
            self.r4[z] = total.astype(BF16)
        elif step == 3:
            total = self.r4[0].astype(F32)
            for k in range(1, 8):
                total = total + self.r4[k].astype(F32)
            done = total.astype(BF16)
            self.res4[...] = done
            self.res2[pl.ds(3 * xy, 3)] = done
        elif step == 4:
            self.out[self.s] = self.res2[...]

    def advance(self, step):
        self.finish(step)
        self.start(step + 1)


def adder_scratch(lanes):
    def of(*dims):
        return pltpu.VMEM((*dims, 16, lanes), BF16)

    return [of(2, 48), of(48), of(48), of(15, 3), of(8, 3), of(3), of(48)]


N_ADDER = 6


def whole_kernel(
    tok, rg, own, gain, wq, wkv, wo, wm, g, gt,
    token_grad, relayed, out_g, out_s,
    *scratch,
):
    (stage, own_tok, region, hstage, hsend, rims, cst, csend, corners, rimst, rimx,
     rows, mg_send, mg_recv, mg, own_send, owners,
     qreg, xreg, kreg, vreg, nreg, norm_n, inv_n, acck, accv, wk, wv,
     abuf, cts, qs, og_e, out_b, out_w, pt, pw, sgs, qbd, qbd_t, cgbd, cgbd_t, ctx_t, qg_t, go, og_n,
     merged, r_merged, kv_h, r_h, kv_c, cstage, r_c, kv_main, r_main, kv_d, r_d,
     normals, kvs, qgs, stage2, wins, wide_out,
     send_sem, recv_sem, g_send, g_recv, s_send, s_recv) = scratch[:68]
    rest = scratch[68:]
    qg_n = qreg
    big = Adder((rest[0], out_g, *rest[1 : 1 + N_ADDER]), g_send, g_recv)
    rest = rest[1 + N_ADDER :]
    small = Adder((rest[0], out_s, *rest[1 : 1 + N_ADDER]), s_send, s_recv)
    s, dep, hei = place()
    peers = neighbours()
    copy = copier(send_sem, recv_sem)
    greeted = list(peers.values()) + big.ps + big.zs
    barrier = pltpu.get_barrier_semaphore()
    for peer in greeted:
        pl.semaphore_signal(barrier, inc=1, device_id=peer, device_id_type=MESH)

    own_send[...] = jnp.full((8, 128), own[0, 0], jnp.int32)
    owners[1] = own_send[...]
    stage[...] = jnp.zeros_like(stage)
    hstage[...] = jnp.zeros_like(hstage)
    cst[...] = jnp.zeros_like(cst)
    for d in range(10):
        x = tok[d].astype(F32)
        stage[d, 1:7, :] = x[0:6]
        stage[d, 9:14, :] = x[5:10]
        stage[d, 8:9, :] = x[4:5]
        hstage[0, d : d + 1, :] = x[0:1]
        hstage[1, d : d + 1, :] = x[9:10]
        if d in (0, 9):
            for side in range(2):
                r = x[9 * side : 9 * side + 1]
                for j in range(15):
                    cst[2 * (d // 9) + side, j : j + 1, :] = r[:, 128 * j : 128 * j + 128]
    own_tok[...] = stage[...].astype(BF16)
    hsend[...] = hstage[...].astype(BF16)
    csend[...] = cst[...].astype(BF16)

    rows[...] = jnp.zeros_like(rows)

    def spread(i, carry):
        x = rg[:, pl.ds(pl.multiple_of(i * 384, 128), 384)].astype(F32)
        for k in range(3):
            rows[k, pl.ds(i, 1), :] = x[k : k + 1]
        return carry

    lax.fori_loop(0, 125, spread, 0)
    acck[...] = jnp.zeros_like(acck)
    accv[...] = jnp.zeros_like(accv)
    qbd_t[...] = jnp.zeros_like(qbd_t)
    cgbd_t[...] = jnp.zeros_like(cgbd_t)
    ones = lax.broadcasted_iota(jnp.int32, (64, 768), 0)
    qbd_t[192:256, :] = jnp.where(ones == 0, 1.0, 0.0).astype(BF16)
    go[...] = jnp.zeros_like(go)
    wk[...] = jnp.zeros_like(wk)
    wk[:, :C] = wkv[:, :C]
    wv[...] = wkv[:, C:]

    def maps(n, carry):
        index = eight_index(n, lax.broadcasted_iota(jnp.int32, (1, 128), 1))
        col = lax.broadcasted_iota(jnp.int32, (1024, 128), 0)
        at = pl.ds(pl.multiple_of(n * 128, 128), 128)
        pt[:, at] = jnp.where(index == col, 1.0, 0.0).astype(BF16)
        index = eight_index(n, lax.broadcasted_iota(jnp.int32, (128, 128), 0))
        col = lax.broadcasted_iota(jnp.int32, (128, 128), 1)
        for o in range(8):
            hit = jnp.where(index == col + 128 * o, 1.0, 0.0).astype(BF16)
            pw[n, :, 128 * o : 128 * o + 128] = hit
        return carry

    lax.fori_loop(0, 8, maps, 0)
    pl.semaphore_wait(barrier, len(greeted))
    to_left = copy(own_send, owners.at[2], 0, peers["sl"])
    to_right = copy(own_send, owners.at[0], 1, peers["sh"])
    far = [
        copy(hsend.at[1], rims.at[0], 5, peers["hh"]),
        copy(hsend.at[0], rims.at[1], 6, peers["hl"]),
        copy(csend.at[3], corners.at[0], 7, peers["hdh"]),
        copy(csend.at[2], corners.at[1], 8, peers["hdl"]),
        copy(csend.at[1], corners.at[2], 9, peers["lh"]),
        copy(csend.at[0], corners.at[3], 10, peers["ll"]),
    ]
    near = [
        copy(own_tok, region.at[pl.ds(1, 10)], 2, peers["p"]),
        copy(own_tok.at[9], region.at[0], 3, peers["dh"]),
        copy(own_tok.at[0], region.at[11], 4, peers["dl"]),
    ]
    to_left.start()
    to_right.start()
    for one in far + near:
        one.start()

    gains = gain[...]
    for pair in range(5):
        lanes = slice(384 * pair, 384 * pair + 384)
        own2 = stage[:, :, lanes].reshape(160, 384)
        for half in range(2):
            w = 2 * pair + half
            x = own2[:, 192 * half : 192 * half + 192]
            normed, inverse = normalized(x)
            norm_n[w] = normed
            inv_n[w] = inverse
            qreg[w] = dot((normed * gains).astype(BF16), wq[...]).reshape(10, 16, C)
            xreg[w] = x.reshape(10, 16, C)
    row = lax.broadcasted_iota(jnp.int32, (192, 256), 0)
    lane = lax.broadcasted_iota(jnp.int32, (192, 256), 1)
    rd, rs = row >> 4, row & 15
    off_depth = ((rd == 0) & (dep == 0)) | ((rd == 11) & (dep == N_DEPTH - 1))
    bias = jnp.where((off_depth | ((rs & 7) == 7)) & (lane == 192), -1e30, 0.0)
    edge = jnp.where(lane == 192, -1e30, 0.0).reshape(12, 16, 256)
    for w in (0, 11):
        kreg[w] = edge
        vreg[w] = jnp.zeros((12, 16, C), F32)

    for one in near:
        one.wait()
    for pair in range(5):
        lanes = slice(384 * pair, 384 * pair + 384)
        reg2 = region[:, :, lanes].astype(F32).reshape(192, 384)
        for half in range(2):
            w = 2 * pair + half
            y = reg2[:, 192 * half : 192 * half + 192]
            normed, _ = normalized(y)
            normal = (normed * gains).astype(BF16)
            nreg[w] = normed.reshape(12, 16, C)
            kreg[w + 1] = (dot(normal, wk[...]) + bias).reshape(12, 16, 256)
            vreg[w + 1] = dot(normal, wv[...]).reshape(12, 16, C)
    to_left.wait()
    to_right.wait()
    fl = jnp.where(owners[0, 0:1, :] == hei, 1, 0)
    fs = jnp.where(owners[1, 0:1, :] == hei, 1, 0)
    fr = jnp.where(owners[2, 0:1, :] == hei, 1, 0)
    rank_l, rank_s, rank_r = relay_ranks(fl, fs, fr)

    def pick_row(rank):
        rank = wide(rank)
        return jnp.where(rank == 0, rows[0], jnp.where(rank == 1, rows[1], rows[2]))

    mg_send[0] = pick_row(rank_l).astype(BF16)
    mg_send[1] = pick_row(rank_r).astype(BF16)
    back = [
        copy(mg_send.at[0], mg_recv.at[1], 11, peers["sl"]),
        copy(mg_send.at[1], mg_recv.at[0], 12, peers["sh"]),
    ]
    for one in back:
        one.start()

    for one in far:
        one.wait()
    rimst[...] = jnp.zeros_like(rimst)
    for side in range(2):
        rimst[side, 1:11, :] = rims[side].astype(F32)[0:10]
        rimst[side, 0:1, :] = lane_row(corners[side].astype(F32))
        rimst[side, 11:12, :] = lane_row(corners[2 + side].astype(F32))
        for pair in range(5):
            x = rimst[side, :, 384 * pair : 384 * pair + 384]
            rimx[side, 2 * pair] = x[:, :C]
            rimx[side, 2 * pair + 1] = x[:, C:]
    rlane = lax.broadcasted_iota(jnp.int32, (160, 256), 1)
    rrow = lax.broadcasted_iota(jnp.int32, (160, 256), 0) & 15
    off_depth = ((rrow == 0) & (dep == 0)) | ((rrow == 11) & (dep == N_DEPTH - 1))
    for side in range(2):
        off = off_depth | (hei == (N_HEIGHT - 1) * side)
        rbias = jnp.where(off & (rlane == 192), -1e30, 0.0)
        normed, _ = normalized(rimx[side].reshape(160, C))
        normal = (normed * gains).astype(BF16)
        kr = (dot(normal, wk[...]) + rbias).reshape(10, 16, 256)
        vr = dot(normal, wv[...]).reshape(10, 16, C)
        nr = normed.reshape(10, 16, C)
        at = slice(14 * side, 14 * side + 1)
        for w in range(10):
            for d in range(12):
                kreg[w + 1, d, at, :] = kr[w, d : d + 1]
                vreg[w + 1, d, at, :] = vr[w, d : d + 1]
                nreg[w, d, at, :] = nr[w, d : d + 1]

    def window_of(i, first):
        hi = (i // 4 + first) % 2
        di, wi = i % 2, (i // 2) % 2
        hs = pl.ds(pl.multiple_of(hi * 8, 8), 8)
        cells = (pl.ds(wi * 5, 5), pl.ds(di * 5, 5), hs, slice(None))
        around = (pl.ds(wi * 5, 7), pl.ds(di * 5, 7), hs, slice(None))
        return wi * 4 + di * 2 + hi, cells, around

    head = lax.broadcasted_iota(jnp.int32, (128, C), 1) >> 5
    odd = hei % 2

    def forward(i, carry):
        n, cells, around = window_of(i, 1 - odd)
        q_w = dot(gt[...], qreg[cells].reshape(200, C).astype(BF16))
        x_w = dot(gt[...], xreg[cells].reshape(200, C).astype(BF16))
        qs[n] = q_w.astype(BF16)
        q_t = q_w.T.astype(BF16)
        for m in range(HEADS):
            r, l = slice(32 * m, 32 * m + 32), slice(128 * m, 128 * m + 128)
            qbd_t[r, l] = q_t[r]
        k = kreg[around].reshape(392, 256).astype(BF16)
        v_t = vreg[around].reshape(392, C).T.astype(BF16)
        for p in range(3):
            l = slice(256 * p, 256 * p + 256)
            e = jnp.exp2(dot(k, qbd_t[:, l]) * EXP2_SCALE)
            a = (e * (1.0 / jnp.sum(e, 0, keepdims=True))).astype(BF16)
            abuf[n, :, l] = a
            c = dot(v_t[64 * p : 64 * p + 64], a)
            ctx_t[64 * p : 64 * p + 32, :] = c[:32, :128]
            ctx_t[64 * p + 32 : 64 * p + 64, :] = c[32:, 128:]
        c_t = ctx_t[...]
        cts[n] = c_t.astype(BF16)
        at = pl.ds(pl.multiple_of(n * 128, 128), 128)
        out_w[at, :] = (dot(c_t.T.astype(BF16), wo[...]) + x_w).astype(BF16)
        return carry

    lax.fori_loop(0, 8, forward, 0)
    total = jnp.zeros((128, 384), F32)
    for o in range(8):
        part = dot(pt[128 * o : 128 * o + 128, :], out_w[...]).astype(BF16)
        out_b[128 * o : 128 * o + 128, :] = part
        total = total + dot(part, wm[192 * o : 192 * o + 192, :])
    merged[...] = total.astype(BF16)
    relays = [
        copy(merged, r_merged.at[1], 13, peers["sl"]),
        copy(merged, r_merged.at[0], 14, peers["sh"]),
    ]
    for one in relays:
        one.start()
    left, right = lax.rem(hei + N_HEIGHT - 1, N_HEIGHT), lax.rem(hei + 1, N_HEIGHT)
    target = wide(owners[1, 0:1, :])
    mine = pick_row(rank_s)
    for one in back:
        one.wait()
    mg[...] = jnp.where(
        target == left,
        mg_recv[0].astype(F32),
        jnp.where(target == right, mg_recv[1].astype(F32), mine),
    ).astype(BF16)
    for o in range(8):
        og_e[128 * o : 128 * o + 128, :] = dot_nt(
            mg[...], wm[192 * o : 192 * o + 192, :]
        ).astype(BF16)

    for o in range(8):
        part = dot_tn(out_b[128 * o : 128 * o + 128, :], mg[...]).astype(BF16)
        big.src[o // 4, 12 * (o % 4) : 12 * (o % 4) + 12] = part.reshape(12, 16, 384)
    big.start(1)
    cstage[...] = jnp.zeros_like(cstage)
    srow = lax.broadcasted_iota(jnp.int32, (16, 192), 0)
    scol = lax.broadcasted_iota(jnp.int32, (16, 192), 1)

    def rim_copies(side):
        hn = lax.rem(hei + 2 * side + N_HEIGHT - 1, N_HEIGHT)
        dl, dh = lax.rem(dep + N_DEPTH - 1, N_DEPTH), lax.rem(dep + 1, N_DEPTH)
        return [
            copy(kv_h.at[side], r_h.at[1 - side], 15 + side, (1 - s, dep, hn)),
            copy(kv_c.at[side], r_c.at[3 - side], 17 + side, (1 - s, dl, hn)),
            copy(kv_c.at[2 + side], r_c.at[1 - side], 19 + side, (1 - s, dh, hn)),
        ]

    def send_rim(side):
        pick = jnp.where(scol == srow * 16 + 14 * side, 1.0, 0.0).astype(BF16)
        for w in range(10):
            t = jnp.concatenate([acck[w + 1], accv[w + 1]], axis=-1)
            r = dot(pick, t.reshape(192, 384).astype(BF16))
            kv_h[side, w] = r.astype(BF16)
            cstage[0, w : w + 1, :] = r[0:1]
            cstage[1, w : w + 1, :] = r[11:12]
        kv_c[side] = cstage[0].astype(BF16)
        kv_c[2 + side] = cstage[1].astype(BF16)
        for one in rim_copies(side):
            one.start()

    def backward(i, carry):
        n, cells, around = window_of(i, odd)
        og_b = dot(pw[n], og_e[...]).astype(BF16)
        cg_w = dot_nt(og_b, wo[...]).astype(BF16).astype(F32)
        q_w = qs[n].astype(F32)
        cg_t = cg_w.T.astype(BF16)
        for m in range(HEADS):
            r, l = slice(32 * m, 32 * m + 32), slice(128 * m, 128 * m + 128)
            cgbd_t[r, l] = cg_t[r]
            qbd[l, :] = jnp.where(head == m, q_w, 0.0).astype(BF16)
            cgbd[l, :] = jnp.where(head == m, cg_w, 0.0).astype(BF16)
        k_t = kreg[around].reshape(392, 256)[:, :C].T.astype(BF16)
        v = vreg[around].reshape(392, C).astype(BF16)
        for p in range(3):
            l = slice(256 * p, 256 * p + 256)
            a = abuf[n, :, l]
            af = a.astype(F32)
            wg = dot(v, cgbd_t[:, l])
            mean = jnp.sum(wg * af, 0, keepdims=True)
            sg = (af * (wg - mean) * SCALE).astype(BF16)
            sgs[:, l] = sg
            c = dot(k_t[64 * p : 64 * p + 64], sg)
            qg_t[64 * p : 64 * p + 32, :] = c[:32, :128]
            qg_t[64 * p + 32 : 64 * p + 64, :] = c[32:, 128:]
        acck[around] += dot(sgs[...], qbd[...]).reshape(7, 7, 8, C)
        accv[around] += dot(abuf[n], cgbd[...]).reshape(7, 7, 8, C)
        go[...] += dot(cts[n], og_b)
        qg_w = qg_t[...].T.astype(BF16)
        qg_n[cells] = dot(g[...], qg_w).reshape(5, 5, 8, C)
        og_n[cells] = dot(g[...], og_b).reshape(5, 5, 8, C)
        for at, step in ((2, 1), (6, 2)):
            pl.when(i == at)(functools.partial(big.advance, step))
        pl.when(i == 3)(functools.partial(send_rim, odd))
        return carry

    lax.fori_loop(0, 8, backward, 0)

    send_rim(1 - odd)
    slot = lax.broadcasted_iota(jnp.int32, (12, 16, 384), 1)
    inner = (slot & 7 >= 1) & (slot & 7 <= 5)
    for w in range(10):
        t = jnp.concatenate([acck[w + 1], accv[w + 1]], axis=-1)
        kvs[192 * w : 192 * w + 192, :] = t.reshape(192, 384).astype(BF16)
        t = t + jnp.where(slot == 5, t[:, 8:9, :], jnp.where(slot == 9, t[:, 6:7, :], 0.0))
        b = jnp.where(inner, t, 0.0).astype(BF16)
        kv_main[w] = b[1:11]
        kv_d[0, w] = b[0]
        kv_d[1, w] = b[11]
    grads = [
        copy(kv_d.at[0], r_d.at[1], 21, peers["dl"]),
        copy(kv_d.at[1], r_d.at[0], 22, peers["dh"]),
        copy(kv_main, r_main, 23, peers["p"]),
    ]
    for one in grads:
        one.start()

    gain_sum = jnp.zeros((1, C), F32)
    for w in range(10):
        normed = nreg[w].reshape(192, C)
        normals[192 * w : 192 * w + 192, :] = (normed * gains).astype(BF16)
        ng = dot_nt(kvs[192 * w : 192 * w + 192, :], wkv[...])
        gain_sum = gain_sum + jnp.sum(ng * normed, 0, keepdims=True)
    part = dot_tn(normals[...], kvs[...]).astype(BF16)
    for j in range(3):
        small.src[0, 12 * j : 12 * j + 12] = part[:, 128 * j : 128 * j + 128].reshape(12, 16, 128)
    for w in range(10):
        normed = norm_n[w]
        normals[160 * w : 160 * w + 160, :] = (normed * gains).astype(BF16)
        qgs[160 * w : 160 * w + 160, :] = qg_n[w].reshape(160, C).astype(BF16)
        ng = dot_nt(qgs[160 * w : 160 * w + 160, :], wq[...])
        xreg[w] = ng.reshape(10, 16, C)
        gain_sum = gain_sum + jnp.sum(ng * normed, 0, keepdims=True)
    part = jnp.concatenate([dot_tn(normals[0:1600, :], qgs[...]), go[...]], axis=1).astype(BF16)
    for j in range(3):
        small.src[1, 12 * j : 12 * j + 12] = part[:, 128 * j : 128 * j + 128].reshape(12, 16, 128)
    first = lax.broadcasted_iota(jnp.int32, (16, 128), 0)
    tail = jnp.concatenate([gain_sum[:, 128:], jnp.zeros((1, 64), F32)], axis=1)
    small.src[:, 36:48] = jnp.zeros((2, 12, 16, 128), BF16)
    small.src[0, 36] = jnp.where(
        first == 0, gain_sum[:, :128], jnp.where(first == 1, tail, 0.0)
    ).astype(BF16)
    small.start(1)

    for one in relays:
        one.wait()
    parts = []
    for flag, rank, win in zip(
        (fl, fs, fr), (rank_l, rank_s, rank_r), (r_merged[0], merged[...], r_merged[1])
    ):
        parts.append((wide(jnp.where(flag == 1, rank, -1)), win.astype(F32)))
    for k in range(3):
        total = jnp.zeros((128, 384), F32)
        for key, win in parts:
            total = jnp.where(key == k, win, total)
        wins[k] = total
    small.advance(1)

    def lay(i, carry):
        lanes = pl.ds(pl.multiple_of(i * 384, 128), 384)
        for k in range(3):
            wide_out[k : k + 1, lanes] = wins[k, pl.ds(i, 1), :]
        return carry

    lax.fori_loop(0, 125, lay, 0)
    relayed[...] = wide_out[...].astype(BF16)
    big.advance(3)
    small.advance(2)
    for one in grads + rim_copies(0) + rim_copies(1):
        one.wait()

    sl = lax.broadcasted_iota(jnp.int32, (16, 384), 0)
    for pair in range(5):
        lanes = slice(384 * pair, 384 * pair + 384)
        found = []
        for half in range(2):
            w = 2 * pair + half
            lo, hi = r_h[0, w].astype(F32), r_h[1, w].astype(F32)
            planes = []
            for d in range(10):
                lo_d, hi_d = lo[d + 1 : d + 2], hi[d + 1 : d + 2]
                if d in (0, 9):
                    e = 2 * (d // 9)
                    lo_d = lo_d + r_c[e].astype(F32)[w : w + 1]
                    hi_d = hi_d + r_c[e + 1].astype(F32)[w : w + 1]
                t = r_main[w, d].astype(F32)
                t = t + jnp.where(sl == 1, lo_d, jnp.where(sl == 13, hi_d, 0.0))
                if d in (0, 9):
                    t = t + r_d[d // 9, w].astype(F32)
                planes.append(t.astype(BF16))
            kv_b = jnp.concatenate(planes, axis=0)
            normed, inverse = norm_n[w], inv_n[w]
            u = (xreg[w].reshape(160, C) + dot_nt(kv_b, wkv[...])) * gains
            found.append(
                inverse
                * (
                    u
                    - jnp.mean(u, -1, keepdims=True)
                    - normed * jnp.mean(u * normed, -1, keepdims=True)
                )
                + og_n[w].reshape(160, C)
            )
        stage[:, :, lanes] = jnp.concatenate(found, axis=1).reshape(10, 16, 384)
        if pair == 2:
            big.advance(4)
            small.advance(3)
    small.advance(4)
    for d in range(10):
        x = stage[d]
        stage2[d, 0:5, :] = x[1:6]
        stage2[d, 5:10, :] = x[9:14]
    token_grad[...] = stage2[...].astype(BF16)
    big.finish(5)
    small.finish(5)


def whole(tok, rg, own, gain, wq, wkv, wo, wm):
    g = np.zeros((200, 128), np.float32)
    for a in range(5):
        for b in range(5):
            for c in range(5):
                g[(a * 5 + b) * 8 + c + 1, a * 25 + b * 5 + c] = 1
    g = jnp.asarray(g, BF16)
    vm, dma = pltpu.VMEM, pltpu.SemaphoreType.DMA
    scratch = [
        vm((10, 16, 1920), F32),
        vm((10, 16, 1920), BF16),
        vm((12, 16, 1920), BF16),
        vm((2, 16, 1920), F32),
        vm((2, 16, 1920), BF16),
        vm((2, 16, 1920), BF16),
        vm((4, 16, 128), F32),
        vm((4, 16, 128), BF16),
        vm((4, 16, 128), BF16),
        vm((2, 16, 1920), F32),
        vm((2, 10, 16, C), F32),
        vm((3, 128, 384), F32),
        vm((2, 128, 384), BF16),
        vm((2, 128, 384), BF16),
        vm((128, 384), BF16),
        vm((8, 128), jnp.int32),
        vm((3, 8, 128), jnp.int32),
        vm((10, 10, 16, C), F32),
        vm((10, 10, 16, C), F32),
        vm((12, 12, 16, 256), F32),
        vm((12, 12, 16, C), F32),
        vm((10, 12, 16, C), F32),
        vm((10, 160, C), F32),
        vm((10, 160, 1), F32),
        vm((12, 12, 16, C), F32),
        vm((12, 12, 16, C), F32),
        vm((C, 256), BF16),
        vm((C, C), BF16),
        vm((8, 392, 768), BF16),
        vm((8, C, 128), BF16),
        vm((8, 128, C), BF16),
        vm((1024, C), BF16),
        vm((1024, C), BF16),
        vm((1024, C), BF16),
        vm((1024, 1024), BF16),
        vm((8, 128, 1024), BF16),
        vm((392, 768), BF16),
        vm((768, C), BF16),
        vm((256, 768), BF16),
        vm((768, C), BF16),
        vm((C, 768), BF16),
        vm((C, 128), F32),
        vm((C, 128), F32),
        vm((C, C), F32),
        vm((10, 10, 16, C), F32),
        vm((128, 384), BF16),
        vm((2, 128, 384), BF16),
        vm((2, 10, 16, 384), BF16),
        vm((2, 10, 16, 384), BF16),
        vm((4, 16, 384), BF16),
        vm((2, 16, 384), F32),
        vm((4, 16, 384), BF16),
        vm((10, 10, 16, 384), BF16),
        vm((10, 10, 16, 384), BF16),
        vm((2, 10, 16, 384), BF16),
        vm((2, 10, 16, 384), BF16),
        vm((1920, C), BF16),
        vm((1920, 384), BF16),
        vm((1600, C), BF16),
        vm((10, 10, 1920), F32),
        vm((3, 128, 384), F32),
        vm((3, 48000), F32),
        dma((24,)), dma((24,)),
        dma((39,)), dma((39,)),
        dma((39,)), dma((39,)),
    ]
    scratch += adder_scratch(384) + adder_scratch(128)
    return pl.pallas_call(
        whole_kernel,
        out_shape=(
            jax.ShapeDtypeStruct((10, 10, 1920), BF16),
            jax.ShapeDtypeStruct((3, 48000), BF16),
            jax.ShapeDtypeStruct((2, 48, 16, 384), BF16),
            jax.ShapeDtypeStruct((2, 48, 16, 128), BF16),
        ),
        in_specs=[VM, VM, SM] + [VM] * 7,
        out_specs=(VM,) * 4,
        scratch_shapes=scratch,
        compiler_params=pltpu.CompilerParams(
            collective_id=1, has_side_effects=True, vmem_limit_bytes=LIMIT
        ),
        name="whole",
    )(tok, rg, own, gain, wq, wkv, wo, wm, g, g.T)


def tail_kernel(
    token_in, relayed_in, big, small, token_grad, relayed, gain, query, keyval, out, merge
):
    scale = (2.0 * 128000) ** (-0.5)
    token_grad[...] = token_in[...]
    relayed[...] = relayed_in[...]
    merge[...] = (big[...].astype(F32) * scale).reshape(1536, 384)

    def joined(half):
        tiles = [
            small[half, 12 * j : 12 * j + 12].astype(F32).reshape(192, 128) for j in range(3)
        ]
        return jnp.concatenate(tiles, axis=1) * scale

    keyval[...] = joined(0)
    both = joined(1)
    query[...] = both[:, :C]
    out[...] = both[:, C:]
    sums = small[0, 36].astype(F32)
    gain[...] = jnp.concatenate([sums[0:1], sums[1:2, : C - 128]], axis=1) * scale


def tail(token_grad, relayed, big, small):
    return pl.pallas_call(
        tail_kernel,
        out_shape=(
            jax.ShapeDtypeStruct((10, 10, 1920), BF16),
            jax.ShapeDtypeStruct((3, 48000), BF16),
            jax.ShapeDtypeStruct((1, C), F32),
            jax.ShapeDtypeStruct((C, C), F32),
            jax.ShapeDtypeStruct((C, 384), F32),
            jax.ShapeDtypeStruct((C, C), F32),
            jax.ShapeDtypeStruct((1536, 384), F32),
        ),
        in_specs=[VM] * 4,
        out_specs=(VM,) * 7,
        compiler_params=pltpu.CompilerParams(vmem_limit_bytes=LIMIT),
        name="tail",
    )(token_grad, relayed, big, small)


def local(tokens, ln_gain, w_query, w_keyval, w_out, w_merge, owner_map, relay_grad):
    results = whole(
        tokens[0], relay_grad[0], owner_map, ln_gain.reshape(1, C), w_query, w_keyval, w_out,
        w_merge,
    )
    token_grad, relayed, gain, query, keyval, out, merge = tail(*results)
    return (relayed[None], token_grad[None], gain.reshape(C), query, keyval, out, merge)


def solution(mesh):
    rows = P("stream", ("depth", "height"), None)
    cells = P("stream", "depth", "height", None)
    return jax.shard_map(
        local,
        mesh=mesh,
        in_specs=(cells, P(), P(), P(), P(), P(), P("depth", "height"), rows),
        out_specs=(rows, cells, P(), P(), P(), P(), P()),
        check_vma=False,
    )
```

```python
import functools

import jax
import jax.numpy as jnp
import numpy as np
from jax import lax
from jax.experimental import pallas as pl
from jax.experimental.pallas import tpu as pltpu
from jax.sharding import PartitionSpec as P

C = 192
HEADS = 6
EPS = 1e-05
N_DEPTH = 4
N_HEIGHT = 32
SCALE = 32 ** (-0.5)
EXP2_SCALE = SCALE * 1.4426950408889634
MESH = pl.DeviceIdType.MESH
F32 = jnp.float32
BF16 = jnp.bfloat16
VM = pl.BlockSpec(memory_space=pltpu.VMEM)
SM = pl.BlockSpec(memory_space=pltpu.SMEM)
LIMIT = 62 * 1024 * 1024


def dot(a, b):
    return lax.dot_general(a, b, (((1,), (0,)), ((), ())), preferred_element_type=F32)


def dot_nt(a, b):
    return lax.dot_general(a, b, (((1,), (1,)), ((), ())), preferred_element_type=F32)


def dot_tn(a, b):
    return lax.dot_general(a, b, (((0,), (0,)), ((), ())), preferred_element_type=F32)


def place():
    return lax.axis_index("stream"), lax.axis_index("depth"), lax.axis_index("height")


def neighbours():
    s, d, h = place()
    dl, dh = lax.rem(d + N_DEPTH - 1, N_DEPTH), lax.rem(d + 1, N_DEPTH)
    hl, hh = lax.rem(h + N_HEIGHT - 1, N_HEIGHT), lax.rem(h + 1, N_HEIGHT)
    o = 1 - s
    return {
        "p": (o, d, h),
        "dl": (o, dl, h),
        "dh": (o, dh, h),
        "hl": (o, d, hl),
        "hh": (o, d, hh),
        "ll": (o, dl, hl),
        "lh": (o, dl, hh),
        "hdl": (o, dh, hl),
        "hdh": (o, dh, hh),
        "sl": (s, d, hl),
        "sh": (s, d, hh),
    }


def greet(peers):
    barrier = pltpu.get_barrier_semaphore()
    for peer in peers:
        pl.semaphore_signal(barrier, inc=1, device_id=peer, device_id_type=MESH)
    pl.semaphore_wait(barrier, len(peers))


def copier(send_sem, recv_sem):
    def make(src, dst, index, peer):
        return pltpu.make_async_remote_copy(
            src_ref=src,
            dst_ref=dst,
            send_sem=send_sem.at[index],
            recv_sem=recv_sem.at[index],
            device_id=peer,
            device_id_type=MESH,
        )

    return make


def relay_ranks(fl, fs, fr):
    _, _, h = place()
    left, right = lax.rem(h + N_HEIGHT - 1, N_HEIGHT), lax.rem(h + 1, N_HEIGHT)

    def before(a, b):
        return jnp.where(a < b, 1, 0)

    rank_l = fs * before(h, left) + fr * before(right, left)
    rank_s = fl * before(left, h) + fr * before(right, h)
    rank_r = fl * before(left, right) + fs * before(h, right)
    return rank_l, rank_s, rank_r


def wide(row):
    return jnp.concatenate([row, row, row], axis=1)


def normalized(x):
    centre = jnp.mean(x, -1, keepdims=True)
    shifted = x - centre
    inverse = lax.rsqrt(jnp.mean(shifted * shifted, -1, keepdims=True) + EPS)
    return shifted * inverse, inverse


def eight_index(window, q):
    wi, di, hi = window // 4, (window // 2) % 2, window % 2
    a = (q * 41) >> 10
    rest = q - a * 25
    b = (rest * 205) >> 10
    c = rest - b * 5
    w, d, h = a + 5 * wi, b + 5 * di, c + 5 * hi
    offset = ((d & 1) * 2 + (h & 1)) * 2 + (w & 1)
    cell = ((d >> 1) * 5 + (h >> 1)) * 5 + (w >> 1)
    return jnp.where(q < 125, offset * 128 + cell, -1)


def lane_row(tile):
    return jnp.concatenate([tile[j : j + 1] for j in range(15)], axis=1)


class Adder:
    def __init__(self, refs, send_sem, recv_sem):
        (self.src, self.out, self.r1, self.snd2, self.r2, self.r4, self.res4,
         self.res2) = refs
        self.copy = copier(send_sem, recv_sem)
        s, d, h = place()
        zh, xy = h // 16, lax.rem(h, 16)
        self.s, self.xy, self.z = s, xy, zh * 4 + d
        self.partner = (1 - s, d, h)
        self.pk = [lax.rem(xy + k, 16) for k in range(1, 16)]
        self.ps = [(s, d, zh * 16 + t) for t in self.pk]
        self.zs = []
        for k in range(1, 8):
            t = lax.rem(self.z + k, 8)
            self.zs.append((s, lax.rem(t, 4), (t // 4) * 16 + xy))

    def copies(self, step):
        c, xy, z = self.copy, self.xy, self.z
        if step == 1:
            return [c(self.src.at[1 - self.s], self.r1, 0, self.partner)]
        if step == 2:
            return [
                c(self.snd2.at[pl.ds(3 * self.pk[k], 3)], self.r2.at[k], 1 + k, self.ps[k])
                for k in range(15)
            ]
        if step == 3:
            return [c(self.r4.at[z], self.r4.at[z], 16 + k, self.zs[k]) for k in range(7)]
        if step == 4:
            at = pl.ds(3 * xy, 3)
            return [c(self.res4, self.res2.at[at], 23 + k, self.ps[k]) for k in range(15)]
        return [c(self.res2, self.out.at[self.s], 38, self.partner)]

    def start(self, step):
        for one in self.copies(step):
            one.start()

    def finish(self, step):
        for one in self.copies(step):
            one.wait()
        xy, z = self.xy, self.z
        if step == 1:
            total = self.src[self.s].astype(F32) + self.r1[...].astype(F32)
            self.snd2[...] = total.astype(BF16)
        elif step == 2:
            at = pl.ds(3 * xy, 3)
            total = self.src[self.s, at].astype(F32) + self.r1[at].astype(F32)
            for k in range(15):
                total = total + self.r2[k].astype(F32)
            self.r4[z] = total.astype(BF16)
        elif step == 3:
            total = self.r4[0].astype(F32)
            for k in range(1, 8):
                total = total + self.r4[k].astype(F32)
            done = total.astype(BF16)
            self.res4[...] = done
            self.res2[pl.ds(3 * xy, 3)] = done
        elif step == 4:
            self.out[self.s] = self.res2[...]

    def advance(self, step):
        self.finish(step)
        self.start(step + 1)


def adder_scratch(lanes):
    def of(*dims):
        return pltpu.VMEM((*dims, 16, lanes), BF16)

    return [of(2, 48), of(48), of(48), of(15, 3), of(8, 3), of(3), of(48)]


N_ADDER = 6


def whole_kernel(
    tok, rg, own, gain, wq, wkv, wo, wm_hbm, g, gt,
    token_grad, relayed, out_g, out_s,
    *scratch,
):
    (stage, own_tok, region, hstage, hsend, rims, cst, csend, corners, rimst, rimx,
     rows, mg_send, mg_recv, mg, own_send, owners,
     qreg, xreg, kreg, vreg, nreg, norm_n, inv_n, acck, accv, wk, wv,
     abuf, cts, qs, og_e, out_b, og_all, cg_all, out_w, pt, pw, sgs, eye, wm, wm_sem, qbd, qbd_t, cgbd, cgbd_t, ctx_t, qg_t, og_n,
     merged, r_merged, kv_h, r_h, kv_c, cstage, r_c, kv_main, r_main, kv_d, r_d,
     normals, kvs, qgs, stage2, wins, wide_out,
     send_sem, recv_sem, g_send, g_recv, s_send, s_recv) = scratch[:72]
    rest = scratch[72:]
    qg_n = qreg
    big = Adder((rest[0], out_g, *rest[1 : 1 + N_ADDER]), g_send, g_recv)
    rest = rest[1 + N_ADDER :]
    small = Adder((rest[0], out_s, *rest[1 : 1 + N_ADDER]), s_send, s_recv)
    s, dep, hei = place()
    peers = neighbours()
    copy = copier(send_sem, recv_sem)
    greeted = list(peers.values()) + big.ps + big.zs
    fetch = pltpu.make_async_copy(wm_hbm, wm, wm_sem)
    fetch.start()
    barrier = pltpu.get_barrier_semaphore()
    for peer in greeted:
        pl.semaphore_signal(barrier, inc=1, device_id=peer, device_id_type=MESH)

    own_send[...] = jnp.full((8, 128), own[0, 0], jnp.int32)
    owners[1] = own_send[...]
    stage[...] = jnp.zeros_like(stage)
    hstage[...] = jnp.zeros_like(hstage)
    cst[...] = jnp.zeros_like(cst)
    for d in range(10):
        x = tok[d].astype(F32)
        stage[d, 1:7, :] = x[0:6]
        stage[d, 9:14, :] = x[5:10]
        stage[d, 8:9, :] = x[4:5]
        hstage[0, d : d + 1, :] = x[0:1]
        hstage[1, d : d + 1, :] = x[9:10]
        if d in (0, 9):
            for side in range(2):
                r = x[9 * side : 9 * side + 1]
                for j in range(15):
                    cst[2 * (d // 9) + side, j : j + 1, :] = r[:, 128 * j : 128 * j + 128]
    own_tok[...] = stage[...].astype(BF16)
    hsend[...] = hstage[...].astype(BF16)
    csend[...] = cst[...].astype(BF16)

    rows[...] = jnp.zeros_like(rows)

    def spread(i, carry):
        x = rg[:, pl.ds(pl.multiple_of(i * 384, 128), 384)].astype(F32)
        for k in range(3):
            rows[k, pl.ds(i, 1), :] = x[k : k + 1]
        return carry

    lax.fori_loop(0, 125, spread, 0, unroll=5)
    acck[...] = jnp.zeros_like(acck)
    accv[...] = jnp.zeros_like(accv)
    qbd_t[...] = jnp.zeros_like(qbd_t)
    cgbd_t[...] = jnp.zeros_like(cgbd_t)
    ones = lax.broadcasted_iota(jnp.int32, (64, 768), 0)
    qbd_t[192:256, :] = jnp.where(ones == 0, 1.0, 0.0).astype(BF16)
    wk[...] = jnp.zeros_like(wk)
    wk[:, :C] = wkv[:, :C]
    wv[...] = wkv[:, C:]

    def maps(n, carry):
        index = eight_index(n, lax.broadcasted_iota(jnp.int32, (1, 128), 1))
        col = lax.broadcasted_iota(jnp.int32, (1024, 128), 0)
        at = pl.ds(pl.multiple_of(n * 128, 128), 128)
        pt[:, at] = jnp.where(index == col, 1.0, 0.0).astype(BF16)
        index = eight_index(n, lax.broadcasted_iota(jnp.int32, (128, 128), 0))
        col = lax.broadcasted_iota(jnp.int32, (128, 128), 1)
        for o in range(8):
            hit = jnp.where(index == col + 128 * o, 1.0, 0.0).astype(BF16)
            pw[at, 128 * o : 128 * o + 128] = hit
        return carry

    lax.fori_loop(0, 8, maps, 0)
    diagonal = lax.broadcasted_iota(jnp.int32, (C, C), 0) == lax.broadcasted_iota(
        jnp.int32, (C, C), 1
    )
    eye[...] = jnp.where(diagonal, 1.0, 0.0).astype(BF16)
    pl.semaphore_wait(barrier, len(greeted))
    to_left = copy(own_send, owners.at[2], 0, peers["sl"])
    to_right = copy(own_send, owners.at[0], 1, peers["sh"])
    far = [
        copy(hsend.at[1], rims.at[0], 5, peers["hh"]),
        copy(hsend.at[0], rims.at[1], 6, peers["hl"]),
        copy(csend.at[3], corners.at[0], 7, peers["hdh"]),
        copy(csend.at[2], corners.at[1], 8, peers["hdl"]),
        copy(csend.at[1], corners.at[2], 9, peers["lh"]),
        copy(csend.at[0], corners.at[3], 10, peers["ll"]),
    ]
    near = [
        copy(own_tok, region.at[pl.ds(1, 10)], 2, peers["p"]),
        copy(own_tok.at[9], region.at[0], 3, peers["dh"]),
        copy(own_tok.at[0], region.at[11], 4, peers["dl"]),
    ]
    to_left.start()
    to_right.start()
    for one in far + near:
        one.start()

    gains = gain[...]
    for pair in range(5):
        lanes = slice(384 * pair, 384 * pair + 384)
        own2 = stage[:, :, lanes].reshape(160, 384)
        for half in range(2):
            w = 2 * pair + half
            x = own2[:, 192 * half : 192 * half + 192]
            normed, inverse = normalized(x)
            norm_n[w] = normed
            inv_n[w] = inverse
            qreg[w] = dot((normed * gains).astype(BF16), wq[...]).reshape(10, 16, C)
            xreg[w] = x.reshape(10, 16, C)
    row = lax.broadcasted_iota(jnp.int32, (192, 256), 0)
    lane = lax.broadcasted_iota(jnp.int32, (192, 256), 1)
    rd, rs = row >> 4, row & 15
    off_depth = ((rd == 0) & (dep == 0)) | ((rd == 11) & (dep == N_DEPTH - 1))
    bias = jnp.where((off_depth | ((rs & 7) == 7)) & (lane == 192), -1e30, 0.0)
    edge = jnp.where(lane == 192, -1e30, 0.0).reshape(12, 16, 256)
    for w in (0, 11):
        kreg[w] = edge
        vreg[w] = jnp.zeros((12, 16, C), F32)

    for one in near:
        one.wait()
    for pair in range(5):
        lanes = slice(384 * pair, 384 * pair + 384)
        reg2 = region[:, :, lanes].astype(F32).reshape(192, 384)
        for half in range(2):
            w = 2 * pair + half
            y = reg2[:, 192 * half : 192 * half + 192]
            normed, _ = normalized(y)
            normal = (normed * gains).astype(BF16)
            nreg[w] = normed.reshape(12, 16, C)
            kreg[w + 1] = (dot(normal, wk[...]) + bias).reshape(12, 16, 256)
            vreg[w + 1] = dot(normal, wv[...]).reshape(12, 16, C)
    to_left.wait()
    to_right.wait()
    fl = jnp.where(owners[0, 0:1, :] == hei, 1, 0)
    fs = jnp.where(owners[1, 0:1, :] == hei, 1, 0)
    fr = jnp.where(owners[2, 0:1, :] == hei, 1, 0)
    rank_l, rank_s, rank_r = relay_ranks(fl, fs, fr)

    def pick_row(rank):
        rank = wide(rank)
        return jnp.where(rank == 0, rows[0], jnp.where(rank == 1, rows[1], rows[2]))

    mg_send[0] = pick_row(rank_l).astype(BF16)
    mg_send[1] = pick_row(rank_r).astype(BF16)
    back = [
        copy(mg_send.at[0], mg_recv.at[1], 11, peers["sl"]),
        copy(mg_send.at[1], mg_recv.at[0], 12, peers["sh"]),
    ]
    for one in back:
        one.start()

    for one in far:
        one.wait()
    rimst[...] = jnp.zeros_like(rimst)
    for side in range(2):
        rimst[side, 1:11, :] = rims[side].astype(F32)[0:10]
        rimst[side, 0:1, :] = lane_row(corners[side].astype(F32))
        rimst[side, 11:12, :] = lane_row(corners[2 + side].astype(F32))
        for pair in range(5):
            x = rimst[side, :, 384 * pair : 384 * pair + 384]
            rimx[side, 2 * pair] = x[:, :C]
            rimx[side, 2 * pair + 1] = x[:, C:]
    rlane = lax.broadcasted_iota(jnp.int32, (160, 256), 1)
    rrow = lax.broadcasted_iota(jnp.int32, (160, 256), 0) & 15
    off_depth = ((rrow == 0) & (dep == 0)) | ((rrow == 11) & (dep == N_DEPTH - 1))
    for side in range(2):
        off = off_depth | (hei == (N_HEIGHT - 1) * side)
        rbias = jnp.where(off & (rlane == 192), -1e30, 0.0)
        normed, _ = normalized(rimx[side].reshape(160, C))
        normal = (normed * gains).astype(BF16)
        kr = (dot(normal, wk[...]) + rbias).reshape(10, 16, 256)
        vr = dot(normal, wv[...]).reshape(10, 16, C)
        nr = normed.reshape(10, 16, C)
        at = slice(14 * side, 14 * side + 1)
        for w in range(10):
            for d in range(12):
                kreg[w + 1, d, at, :] = kr[w, d : d + 1]
                vreg[w + 1, d, at, :] = vr[w, d : d + 1]
                nreg[w, d, at, :] = nr[w, d : d + 1]

    def window_of(i, first):
        hi = (i // 4 + first) % 2
        di, wi = i % 2, (i // 2) % 2
        hs = pl.ds(pl.multiple_of(hi * 8, 8), 8)
        cells = (pl.ds(wi * 5, 5), pl.ds(di * 5, 5), hs, slice(None))
        around = (pl.ds(wi * 5, 7), pl.ds(di * 5, 7), hs, slice(None))
        return wi * 4 + di * 2 + hi, cells, around

    head = lax.broadcasted_iota(jnp.int32, (128, C), 1) >> 5
    odd = hei % 2

    def forward(i, carry):
        n, cells, around = window_of(i, 1 - odd)
        q_w = dot(gt[...], qreg[cells].reshape(200, C).astype(BF16))
        x_w = dot(gt[...], xreg[cells].reshape(200, C).astype(BF16))
        qs[n] = q_w.astype(BF16)
        q_t = q_w.T.astype(BF16)
        for m in range(HEADS):
            r, l = slice(32 * m, 32 * m + 32), slice(128 * m, 128 * m + 128)
            qbd_t[r, l] = q_t[r]
        k = kreg[around].reshape(392, 256).astype(BF16)
        v_t = dot_nt(eye[...], vreg[around].reshape(392, C).astype(BF16)).astype(BF16)
        for p in range(3):
            l = slice(256 * p, 256 * p + 256)
            e = jnp.exp2(dot(k, qbd_t[:, l]) * EXP2_SCALE)
            a = (e * (1.0 / jnp.sum(e, 0, keepdims=True))).astype(BF16)
            abuf[n, :, l] = a
            c = dot(v_t[64 * p : 64 * p + 64], a)
            ctx_t[64 * p : 64 * p + 32, :] = c[:32, :128]
            ctx_t[64 * p + 32 : 64 * p + 64, :] = c[32:, 128:]
        c_t = ctx_t[...]
        at = pl.ds(pl.multiple_of(n * 128, 128), 128)
        cts[:, at] = c_t.astype(BF16)
        out_w[at, :] = (dot(c_t.T.astype(BF16), wo[...]) + x_w).astype(BF16)
        return carry

    lax.fori_loop(0, 8, forward, 0, unroll=2)
    fetch.wait()
    total = jnp.zeros((128, 384), F32)
    for o in range(8):
        part = dot(pt[128 * o : 128 * o + 128, :], out_w[...]).astype(BF16)
        out_b[128 * o : 128 * o + 128, :] = part
        total = total + dot(part, wm[192 * o : 192 * o + 192, :])
    merged[...] = total.astype(BF16)
    relays = [
        copy(merged, r_merged.at[1], 13, peers["sl"]),
        copy(merged, r_merged.at[0], 14, peers["sh"]),
    ]
    for one in relays:
        one.start()
    left, right = lax.rem(hei + N_HEIGHT - 1, N_HEIGHT), lax.rem(hei + 1, N_HEIGHT)
    target = wide(owners[1, 0:1, :])
    mine = pick_row(rank_s)
    for one in back:
        one.wait()
    mg[...] = jnp.where(
        target == left,
        mg_recv[0].astype(F32),
        jnp.where(target == right, mg_recv[1].astype(F32), mine),
    ).astype(BF16)
    for o in range(8):
        og_e[128 * o : 128 * o + 128, :] = dot_nt(
            mg[...], wm[192 * o : 192 * o + 192, :]
        ).astype(BF16)

    og_all[...] = dot(pw[...], og_e[...]).astype(BF16)
    cg_all[...] = dot_nt(og_all[...], wo[...]).astype(BF16)
    for o in range(8):
        part = dot_tn(out_b[128 * o : 128 * o + 128, :], mg[...]).astype(BF16)
        big.src[o // 4, 12 * (o % 4) : 12 * (o % 4) + 12] = part.reshape(12, 16, 384)
    big.start(1)
    cstage[...] = jnp.zeros_like(cstage)
    srow = lax.broadcasted_iota(jnp.int32, (16, 192), 0)
    scol = lax.broadcasted_iota(jnp.int32, (16, 192), 1)

    def rim_copies(side):
        hn = lax.rem(hei + 2 * side + N_HEIGHT - 1, N_HEIGHT)
        dl, dh = lax.rem(dep + N_DEPTH - 1, N_DEPTH), lax.rem(dep + 1, N_DEPTH)
        return [
            copy(kv_h.at[side], r_h.at[1 - side], 15 + side, (1 - s, dep, hn)),
            copy(kv_c.at[side], r_c.at[3 - side], 17 + side, (1 - s, dl, hn)),
            copy(kv_c.at[2 + side], r_c.at[1 - side], 19 + side, (1 - s, dh, hn)),
        ]

    def send_rim(side):
        pick = jnp.where(scol == srow * 16 + 14 * side, 1.0, 0.0).astype(BF16)
        for w in range(10):
            t = jnp.concatenate([acck[w + 1], accv[w + 1]], axis=-1)
            r = dot(pick, t.reshape(192, 384).astype(BF16))
            kv_h[side, w] = r.astype(BF16)
            cstage[0, w : w + 1, :] = r[0:1]
            cstage[1, w : w + 1, :] = r[11:12]
        kv_c[side] = cstage[0].astype(BF16)
        kv_c[2 + side] = cstage[1].astype(BF16)
        for one in rim_copies(side):
            one.start()

    def backward(i, carry):
        n, cells, around = window_of(i, odd)
        at = pl.ds(pl.multiple_of(n * 128, 128), 128)
        og_b = og_all[at, :]
        cg_w = cg_all[at, :].astype(F32)
        q_w = qs[n].astype(F32)
        cg_t = cg_w.T.astype(BF16)
        for m in range(HEADS):
            r, l = slice(32 * m, 32 * m + 32), slice(128 * m, 128 * m + 128)
            cgbd_t[r, l] = cg_t[r]
            qbd[l, :] = jnp.where(head == m, q_w, 0.0).astype(BF16)
            cgbd[l, :] = jnp.where(head == m, cg_w, 0.0).astype(BF16)
        k_t = dot_nt(eye[...], kreg[around].reshape(392, 256)[:, :C].astype(BF16)).astype(BF16)
        v = vreg[around].reshape(392, C).astype(BF16)
        for p in range(3):
            l = slice(256 * p, 256 * p + 256)
            a = abuf[n, :, l]
            af = a.astype(F32)
            wg = dot(v, cgbd_t[:, l])
            mean = jnp.sum(wg * af, 0, keepdims=True)
            sg = (af * (wg - mean) * SCALE).astype(BF16)
            sgs[:, l] = sg
            c = dot(k_t[64 * p : 64 * p + 64], sg)
            qg_t[64 * p : 64 * p + 32, :] = c[:32, :128]
            qg_t[64 * p + 32 : 64 * p + 64, :] = c[32:, 128:]
        acck[around] += dot(sgs[...], qbd[...]).reshape(7, 7, 8, C)
        accv[around] += dot(abuf[n], cgbd[...]).reshape(7, 7, 8, C)
        qg_w = qg_t[...].T.astype(BF16)
        qg_n[cells] = dot(g[...], qg_w).reshape(5, 5, 8, C)
        og_n[cells] = dot(g[...], og_b).reshape(5, 5, 8, C)
        for at, step in ((2, 1), (6, 2)):
            pl.when(i == at)(functools.partial(big.advance, step))
        pl.when(i == 3)(functools.partial(send_rim, odd))
        return carry

    lax.fori_loop(0, 8, backward, 0)

    send_rim(1 - odd)
    slot = lax.broadcasted_iota(jnp.int32, (12, 16, 384), 1)
    inner = (slot & 7 >= 1) & (slot & 7 <= 5)
    for w in range(10):
        t = jnp.concatenate([acck[w + 1], accv[w + 1]], axis=-1)
        kvs[192 * w : 192 * w + 192, :] = t.reshape(192, 384).astype(BF16)
        t = t + jnp.where(slot == 5, t[:, 8:9, :], jnp.where(slot == 9, t[:, 6:7, :], 0.0))
        b = jnp.where(inner, t, 0.0).astype(BF16)
        kv_main[w] = b[1:11]
        kv_d[0, w] = b[0]
        kv_d[1, w] = b[11]
    grads = [
        copy(kv_d.at[0], r_d.at[1], 21, peers["dl"]),
        copy(kv_d.at[1], r_d.at[0], 22, peers["dh"]),
        copy(kv_main, r_main, 23, peers["p"]),
    ]
    for one in grads:
        one.start()

    gain_sum = jnp.zeros((1, C), F32)
    for w in range(10):
        normed = nreg[w].reshape(192, C)
        normals[192 * w : 192 * w + 192, :] = (normed * gains).astype(BF16)
        ng = dot_nt(kvs[192 * w : 192 * w + 192, :], wkv[...])
        gain_sum = gain_sum + jnp.sum(ng * normed, 0, keepdims=True)
    part = dot_tn(normals[...], kvs[...]).astype(BF16)
    for j in range(3):
        small.src[0, 12 * j : 12 * j + 12] = part[:, 128 * j : 128 * j + 128].reshape(12, 16, 128)
    for w in range(10):
        normed = norm_n[w]
        normals[160 * w : 160 * w + 160, :] = (normed * gains).astype(BF16)
        qgs[160 * w : 160 * w + 160, :] = qg_n[w].reshape(160, C).astype(BF16)
        ng = dot_nt(qgs[160 * w : 160 * w + 160, :], wq[...])
        xreg[w] = ng.reshape(10, 16, C)
        gain_sum = gain_sum + jnp.sum(ng * normed, 0, keepdims=True)
    part = jnp.concatenate([dot_tn(normals[0:1600, :], qgs[...]), dot(cts[...], og_all[...])], axis=1).astype(BF16)
    for j in range(3):
        small.src[1, 12 * j : 12 * j + 12] = part[:, 128 * j : 128 * j + 128].reshape(12, 16, 128)
    first = lax.broadcasted_iota(jnp.int32, (16, 128), 0)
    tail = jnp.concatenate([gain_sum[:, 128:], jnp.zeros((1, 64), F32)], axis=1)
    small.src[:, 36:48] = jnp.zeros((2, 12, 16, 128), BF16)
    small.src[0, 36] = jnp.where(
        first == 0, gain_sum[:, :128], jnp.where(first == 1, tail, 0.0)
    ).astype(BF16)
    small.start(1)

    for one in relays:
        one.wait()
    parts = []
    for flag, rank, win in zip(
        (fl, fs, fr), (rank_l, rank_s, rank_r), (r_merged[0], merged[...], r_merged[1])
    ):
        parts.append((wide(jnp.where(flag == 1, rank, -1)), win.astype(F32)))
    for k in range(3):
        total = jnp.zeros((128, 384), F32)
        for key, win in parts:
            total = jnp.where(key == k, win, total)
        wins[k] = total
    small.advance(1)

    def lay(i, carry):
        lanes = pl.ds(pl.multiple_of(i * 384, 128), 384)
        for k in range(3):
            wide_out[k : k + 1, lanes] = wins[k, pl.ds(i, 1), :]
        return carry

    lax.fori_loop(0, 125, lay, 0, unroll=5)
    relayed[...] = wide_out[...].astype(BF16)
    big.advance(3)
    small.advance(2)
    for one in grads + rim_copies(0) + rim_copies(1):
        one.wait()

    sl = lax.broadcasted_iota(jnp.int32, (16, 384), 0)
    for pair in range(5):
        lanes = slice(384 * pair, 384 * pair + 384)
        found = []
        for half in range(2):
            w = 2 * pair + half
            lo, hi = r_h[0, w].astype(F32), r_h[1, w].astype(F32)
            planes = []
            for d in range(10):
                lo_d, hi_d = lo[d + 1 : d + 2], hi[d + 1 : d + 2]
                if d in (0, 9):
                    e = 2 * (d // 9)
                    lo_d = lo_d + r_c[e].astype(F32)[w : w + 1]
                    hi_d = hi_d + r_c[e + 1].astype(F32)[w : w + 1]
                t = r_main[w, d].astype(F32)
                t = t + jnp.where(sl == 1, lo_d, jnp.where(sl == 13, hi_d, 0.0))
                if d in (0, 9):
                    t = t + r_d[d // 9, w].astype(F32)
                planes.append(t.astype(BF16))
            kv_b = jnp.concatenate(planes, axis=0)
            normed, inverse = norm_n[w], inv_n[w]
            u = (xreg[w].reshape(160, C) + dot_nt(kv_b, wkv[...])) * gains
            found.append(
                inverse
                * (
                    u
                    - jnp.mean(u, -1, keepdims=True)
                    - normed * jnp.mean(u * normed, -1, keepdims=True)
                )
                + og_n[w].reshape(160, C)
            )
        stage[:, :, lanes] = jnp.concatenate(found, axis=1).reshape(10, 16, 384)
        if pair == 2:
            big.advance(4)
            small.advance(3)
    small.advance(4)
    for d in range(10):
        x = stage[d]
        stage2[d, 0:5, :] = x[1:6]
        stage2[d, 5:10, :] = x[9:14]
    token_grad[...] = stage2[...].astype(BF16)
    big.finish(5)
    small.finish(5)


def whole(tok, rg, own, gain, wq, wkv, wo, wm):
    g = np.zeros((200, 128), np.float32)
    for a in range(5):
        for b in range(5):
            for c in range(5):
                g[(a * 5 + b) * 8 + c + 1, a * 25 + b * 5 + c] = 1
    g = jnp.asarray(g, BF16)
    vm, dma = pltpu.VMEM, pltpu.SemaphoreType.DMA
    scratch = [
        vm((10, 16, 1920), F32),
        vm((10, 16, 1920), BF16),
        vm((12, 16, 1920), BF16),
        vm((2, 16, 1920), F32),
        vm((2, 16, 1920), BF16),
        vm((2, 16, 1920), BF16),
        vm((4, 16, 128), F32),
        vm((4, 16, 128), BF16),
        vm((4, 16, 128), BF16),
        vm((2, 16, 1920), F32),
        vm((2, 10, 16, C), F32),
        vm((3, 128, 384), F32),
        vm((2, 128, 384), BF16),
        vm((2, 128, 384), BF16),
        vm((128, 384), BF16),
        vm((8, 128), jnp.int32),
        vm((3, 8, 128), jnp.int32),
        vm((10, 10, 16, C), F32),
        vm((10, 10, 16, C), F32),
        vm((12, 12, 16, 256), F32),
        vm((12, 12, 16, C), F32),
        vm((10, 12, 16, C), F32),
        vm((10, 160, C), F32),
        vm((10, 160, 1), F32),
        vm((12, 12, 16, C), F32),
        vm((12, 12, 16, C), F32),
        vm((C, 256), BF16),
        vm((C, C), BF16),
        vm((8, 392, 768), BF16),
        vm((C, 1024), BF16),
        vm((8, 128, C), BF16),
        vm((1024, C), BF16),
        vm((1024, C), BF16),
        vm((1024, C), BF16),
        vm((1024, C), BF16),
        vm((1024, C), BF16),
        vm((1024, 1024), BF16),
        vm((1024, 1024), BF16),
        vm((392, 768), BF16),
        vm((C, C), BF16),
        vm((1536, 384), BF16),
        dma(()),
        vm((768, C), BF16),
        vm((256, 768), BF16),
        vm((768, C), BF16),
        vm((C, 768), BF16),
        vm((C, 128), F32),
        vm((C, 128), F32),
        vm((10, 10, 16, C), F32),
        vm((128, 384), BF16),
        vm((2, 128, 384), BF16),
        vm((2, 10, 16, 384), BF16),
        vm((2, 10, 16, 384), BF16),
        vm((4, 16, 384), BF16),
        vm((2, 16, 384), F32),
        vm((4, 16, 384), BF16),
        vm((10, 10, 16, 384), BF16),
        vm((10, 10, 16, 384), BF16),
        vm((2, 10, 16, 384), BF16),
        vm((2, 10, 16, 384), BF16),
        vm((1920, C), BF16),
        vm((1920, 384), BF16),
        vm((1600, C), BF16),
        vm((10, 10, 1920), F32),
        vm((3, 128, 384), F32),
        vm((3, 48000), F32),
        dma((24,)), dma((24,)),
        dma((39,)), dma((39,)),
        dma((39,)), dma((39,)),
    ]
    scratch += adder_scratch(384) + adder_scratch(128)
    return pl.pallas_call(
        whole_kernel,
        out_shape=(
            jax.ShapeDtypeStruct((10, 10, 1920), BF16),
            jax.ShapeDtypeStruct((3, 48000), BF16),
            jax.ShapeDtypeStruct((2, 48, 16, 384), BF16),
            jax.ShapeDtypeStruct((2, 48, 16, 128), BF16),
        ),
        in_specs=[VM, VM, SM] + [VM] * 4 + [pl.BlockSpec(memory_space=pl.ANY)] + [VM] * 2,
        out_specs=(VM,) * 4,
        scratch_shapes=scratch,
        compiler_params=pltpu.CompilerParams(
            collective_id=1, has_side_effects=True, vmem_limit_bytes=LIMIT
        ),
        name="whole",
    )(tok, rg, own, gain, wq, wkv, wo, wm, g, g.T)


def tail_kernel(
    token_in, relayed_in, big, small, token_grad, relayed, gain, query, keyval, out, merge
):
    scale = (2.0 * 128000) ** (-0.5)
    token_grad[...] = token_in[...]
    relayed[...] = relayed_in[...]
    merge[...] = (big[...].astype(F32) * scale).reshape(1536, 384)

    def joined(half):
        tiles = [
            small[half, 12 * j : 12 * j + 12].astype(F32).reshape(192, 128) for j in range(3)
        ]
        return jnp.concatenate(tiles, axis=1) * scale

    keyval[...] = joined(0)
    both = joined(1)
    query[...] = both[:, :C]
    out[...] = both[:, C:]
    sums = small[0, 36].astype(F32)
    gain[...] = jnp.concatenate([sums[0:1], sums[1:2, : C - 128]], axis=1) * scale


def tail(token_grad, relayed, big, small):
    return pl.pallas_call(
        tail_kernel,
        out_shape=(
            jax.ShapeDtypeStruct((10, 10, 1920), BF16),
            jax.ShapeDtypeStruct((3, 48000), BF16),
            jax.ShapeDtypeStruct((1, C), F32),
            jax.ShapeDtypeStruct((C, C), F32),
            jax.ShapeDtypeStruct((C, 384), F32),
            jax.ShapeDtypeStruct((C, C), F32),
            jax.ShapeDtypeStruct((1536, 384), F32),
        ),
        in_specs=[VM] * 4,
        out_specs=(VM,) * 7,
        compiler_params=pltpu.CompilerParams(vmem_limit_bytes=LIMIT),
        name="tail",
    )(token_grad, relayed, big, small)


def local(tokens, ln_gain, w_query, w_keyval, w_out, w_merge, owner_map, relay_grad):
    results = whole(
        tokens[0], relay_grad[0], owner_map, ln_gain.reshape(1, C), w_query, w_keyval, w_out,
        w_merge,
    )
    token_grad, relayed, gain, query, keyval, out, merge = tail(*results)
    return (relayed[None], token_grad[None], gain.reshape(C), query, keyval, out, merge)


def solution(mesh):
    rows = P("stream", ("depth", "height"), None)
    cells = P("stream", "depth", "height", None)
    return jax.shard_map(
        local,
        mesh=mesh,
        in_specs=(cells, P(), P(), P(), P(), P(), P("depth", "height"), rows),
        out_specs=(rows, cells, P(), P(), P(), P(), P()),
        check_vma=False,
    )
```
